512 devices in a mesh: grp: 16 (over z_hi, y, core), col: 32 (over z_lo, x).
Axes of the slice: x: 4, y: 4, z: 16 (z_hi: 2, z_lo: 8; z = z_hi * 8 + z_lo), core: 2. Of those that a mesh axis runs over, the one named last changes fastest.
Arguments:
- blocks: bfloat16 [8192, 320, 320], P(('grp', 'col')), may hold values from -0.3125 to 0.3125
- block_row: int32 [8192], P(('grp', 'col')), may hold values from 0 to 2047, as said below
- block_col: int32 [8192], P(('grp', 'col')), may hold values from 0 to 2047, as said below
- panel_owner: int32 [2], replicated, may hold values from 0 to 31, as said below
- basis: bfloat16 [2048, 320, 512], P(('grp', 'col')), may hold values from -0.1484375 to 0.1484375
Outputs:
- reduced: float32 [512, 2, 512], P('col')
The draws below stay inside these ranges and needn't reach their ends.
Inputs may be any that keep to these rules, and one draw needn't show every extreme that they name: `block_row`: the blocks of device position d (blocks d * 16 onward) have row clusters among d * 4 to d * 4 + 3 and column clusters in the same row group; they come in 2 runs of 8 blocks, run s holding exactly the device's blocks of window step s (panel column panel_owner[s]); no two blocks of one device share both row and column cluster. `block_col`: see block_row. `panel_owner`: entries are distinct.
All inputs are finite; a program needn't handle non-finite values.
Results may differ from the reference program's by a relative error of at most 0.0029.
Values may be sent and summed in bfloat16 or wider, within the bound.
A program may use at most 64 MiB of HBM per device.

```python
import jax
import jax.numpy as jnp
from jax import lax

BS = 320
MODES = 512
STEPS = 2
CL_DEV = 4
BLK_DEV = 16
CLUSTERS = 2048
BLOCKS = 8192
N_GRP = 16
N_COL = 32


def layout(key):
    device_count = N_GRP * N_COL
    per_step = BLK_DEV // STEPS
    picked = jax.random.permutation(jax.random.fold_in(key, 11), N_COL)[:STEPS].astype(jnp.int32)
    has_last = jnp.any(picked == N_COL - 1)
    forced_slot = jax.random.randint(jax.random.fold_in(key, 13), (), 0, STEPS)
    forced = picked.at[forced_slot].set(N_COL - 1)
    owners = jnp.where(has_last, picked, forced).astype(jnp.int32)
    run_keys = jax.random.split(jax.random.fold_in(key, 12), device_count * STEPS)
    slot_ids = jax.vmap(lambda one_key: jax.random.permutation(one_key, CL_DEV * CL_DEV)[:per_step])(run_keys)
    slot_ids = slot_ids.astype(jnp.int32)
    row_slot = slot_ids // CL_DEV
    col_slot = slot_ids % CL_DEV
    row_slot = (row_slot + (CL_DEV - 1) - row_slot[:, :1]) % CL_DEV
    col_slot = (col_slot + (CL_DEV - 1) - col_slot[:, :1]) % CL_DEV
    row_slot = row_slot.reshape(device_count, STEPS * per_step).astype(jnp.int32)
    col_slot = col_slot.reshape(device_count, STEPS * per_step).astype(jnp.int32)
    step_slot = jnp.repeat(jnp.arange(STEPS, dtype=jnp.int32), per_step)[None, :]
    device = jnp.arange(device_count, dtype=jnp.int32)[:, None]
    row_ids = device * CL_DEV + row_slot
    group_id = device // N_COL
    col_ids = (group_id * N_COL + owners[step_slot]) * CL_DEV + col_slot
    return (row_ids.reshape(-1).astype(jnp.int32), col_ids.reshape(-1).astype(jnp.int32), owners)


def draw_block_row(key, part):
    return layout(key)[0]


def draw_block_col(key, part):
    return layout(key)[1]


def draw_panel_owner(key, part):
    return layout(key)[2]


def level_of(rng, shape, shards, smallest, top_value):
    def one(dim, shards_of):
        heights = jax.random.uniform(jax.random.fold_in(jax.random.fold_in(rng, 6), dim), (shards_of,), jnp.float32, smallest / len(shards), top_value / len(shards))
        return jnp.repeat(jnp.exp(heights), shape[dim] // shards_of).reshape((-1,) + (1,) * (len(shape) - dim - 1))

    level = one(*shards[0])
    for cut in shards[1:]:
        level = level * one(*cut)
    return level


def noise(own_key, dims, spread, reach, cuts=(), kind=jnp.bfloat16):
    result = spread * jax.random.normal(own_key, dims, jnp.float32)
    if cuts:
        result = result * level_of(own_key, dims, cuts, -0.22, 0.18)
    return jnp.clip(result, -reach, reach).astype(kind)


def setup_inputs(seed: int = 0) -> dict:
    key_list = jax.random.split(jax.random.key(seed), 6)
    return {
        "blocks": noise(key_list[0], (BLOCKS, BS, BS), BS ** -0.5, 0.3125, ((0, 512),)),
        "block_row": draw_block_row(jax.random.fold_in(key_list[5], 71), 0),
        "block_col": draw_block_col(jax.random.fold_in(key_list[5], 71), 0),
        "panel_owner": draw_panel_owner(jax.random.fold_in(key_list[5], 71), 0),
        "basis": noise(key_list[4], (CLUSTERS, BS, MODES), (1.0 / (4 * CLUSTERS * BS) ** 0.25), 0.1484375, ((0, 512),)),
    }


def reference(blocks, block_row, block_col, panel_owner, basis):
    device_count = N_GRP * N_COL
    blocks_dev = blocks.reshape(device_count, BLK_DEV, BS, BS)
    rows_dev = block_row.reshape(device_count, BLK_DEV)
    cols_dev = block_col.reshape(device_count, BLK_DEV)
    basis_dev = basis.reshape(device_count, CL_DEV, BS, MODES)
    cluster_ids = jnp.arange(CL_DEV, dtype=jnp.int32)

    def device_term(summed, pieces):
        blk, row_ids, col_ids, own_basis = pieces
        chosen = jnp.take(basis, col_ids, axis=0)
        products = jnp.einsum("bij,bjm->bim", blk.astype(jnp.float32), chosen.astype(jnp.float32))
        local_row = row_ids % CL_DEV
        panel_column = (col_ids // CL_DEV) % N_COL
        row_onehot = (local_row[None, :] == cluster_ids[:, None]).astype(jnp.float32)
        step_mask = (panel_column[None, :] == panel_owner[:, None]).astype(jnp.float32)
        weights = step_mask[:, None, :] * row_onehot[None, :, :]
        panel_rows = jnp.einsum("srb,bim->srim", weights, products, precision=lax.Precision.HIGHEST).astype(jnp.bfloat16)
        term = jnp.einsum("cim,scin->msn", own_basis.astype(jnp.float32), panel_rows.astype(jnp.float32))
        return summed + term, None

    start_sum = jnp.zeros((MODES, STEPS, MODES), jnp.float32)
    summed, unused = lax.scan(device_term, start_sum, (blocks_dev, rows_dev, cols_dev, basis_dev))
    return summed
```

```python
import jax
import jax.numpy as jnp
from jax import lax
from jax.experimental import pallas as pl
from jax.experimental.pallas import tpu as pltpu
from jax.sharding import PartitionSpec as P

X, Y, Z, ZH, CORES = 4, 4, 8, 2, 2
RING = Z * ZH
BS, MODES, STEPS, CL, RUN = 320, 512, 2, 4, 8
PAD = 384
CHUNKS = 10
CH = BS // CHUNKS
PIECES = 10
PC = BS // PIECES
PH = PC // 2
T = STEPS * CHUNKS
G = STEPS * PIECES
SKEW = 3
AHEAD = 4
LEAD = 3
LAG = 3
COLS = X * Z
NH = 2
BF, F32 = jnp.bfloat16, jnp.float32


class Here:
    def __init__(self):
        grp, col = lax.axis_index("grp"), lax.axis_index("col")
        self.core, self.y, self.zh = grp % CORES, (grp // CORES) % Y, grp // (CORES * Y)
        self.z, self.x = col // X, col % X
        self.zg = self.zh * Z + self.z

    def at(self, zh=None, y=None, core=None, z=None, x=None):
        zh = self.zh if zh is None else zh
        y = self.y if y is None else y
        core = self.core if core is None else core
        z = self.z if z is None else z
        x = self.x if x is None else x
        return ((zh * Y + y) * CORES + core, z * X + x)

    def ring(self, d):
        p = (self.zg + d) % RING
        return self.at(zh=p // Z, z=p % Z)


def send(src, dst, ssem, rsem, dev):
    pltpu.make_async_remote_copy(
        src_ref=src, dst_ref=dst, send_sem=ssem, recv_sem=rsem,
        device_id=dev, device_id_type=pl.DeviceIdType.MESH,
    ).start()


def drain(ref, sem):
    pltpu.make_async_copy(ref, ref, sem).wait()


def meet(peers):
    barrier = pltpu.get_barrier_semaphore()
    for dev in peers:
        pl.semaphore_signal(barrier, inc=1, device_id=dev, device_id_type=pl.DeviceIdType.MESH)
    pl.semaphore_wait(barrier, len(peers))


def body(
    owner, brow, bcol, basis, blocks, out,
    blk, dense, basis_t, tsp, got, tr, tl, up_in, dn_in, up_out, dn_out, pan,
    share, core_in, mine, theirs, b3, z_in, out_all,
    blk_sem, s_x, s_tr, s_rl, s_z, s_ag, s_fw, s_core, s_p, s_zz, s_out,
    r_right, r_left, r_tr, r_tl, r_fr, r_fl, r_up, r_dn, r_ar, r_al, r_br, r_bl,
    r_core, r_p, r_zz, r_out,
):
    here = Here()
    core, x, y, z, zh, zg, at, ring = here.core, here.x, here.y, here.z, here.zh, here.zg, here.at, here.ring
    xr, xl, xo = (x + 1) % X, (x + 3) % X, (x + 2) % X
    right, left = at(x=xr), at(x=xl)
    above, below = at(z=(z + 1) % Z), at(z=(z + Z - 1) % Z)
    plane = [(dx, dy) for dx in range(X) for dy in range(Y) if dx or dy]
    copies = [(dh, dy, dc) for dh in range(ZH) for dy in range(Y) for dc in range(CORES) if dh or dy or dc]

    fetch = pltpu.make_async_copy(blocks, blk, blk_sem)
    fetch.start()

    def copy_at(dh, dy, dc):
        return (zh + dh) % ZH, (y + dy) % Y, (core + dc) % CORES

    peers = [at(x=(x + dx) % X, y=(y + dy) % Y) for dx, dy in plane]
    peers += [ring(d) for d in range(1, RING)]
    for dh, dy, dc in copies:
        if dc or (dh and dy):
            hh, yy, cc = copy_at(dh, dy, dc)
            peers.append(at(zh=hh, y=yy, core=cc))
    meet(peers)

    def piece(k):
        start = k * PC
        return (
            pl.ds(pl.multiple_of(start, PC), PC),
            pl.ds(pl.multiple_of(start, PH), PH),
            pl.ds(pl.multiple_of(start + PH, PH), PH),
            pl.ds(pl.multiple_of(k * PH, PH), PH),
        )

    def offer(k):
        rows, first, second, half = piece(k)
        send(basis.at[xo, first], tr.at[half], s_tr.at[0], r_tr.at[k], right)
        send(basis.at[xo, second], tl.at[half], s_tr.at[1], r_tl.at[k], left)
        send(basis.at[xr, rows], got.at[3, rows], s_x.at[0], r_right.at[k], right)
        send(basis.at[xl, rows], got.at[1, rows], s_x.at[1], r_left.at[k], left)

    for k in range(AHEAD):
        offer(k)
    got[0] = basis[x]
    for c in range(CL):
        pads = slice(c * PAD + BS, (c + 1) * PAD)
        basis_t[:, pads] = jnp.zeros((MODES, PAD - BS), BF)
        for s in range(STEPS):
            pan[s, c, BS:] = jnp.zeros((PAD - BS, MODES), BF)
            tsp[s, pads] = jnp.zeros((PAD - BS, MODES), BF)
            dense[s, :, pads] = jnp.zeros((CL * BS, PAD - BS), BF)

    def turn(i):
        c, m = i // CL, i % CL
        lanes = pl.ds(pl.multiple_of(m * 128, 128), 128)
        piece = basis[c, :, lanes].astype(F32).T.astype(BF)
        basis_t[lanes, pl.ds(pl.multiple_of(c * PAD, PAD), BS)] = piece

    def place(i):
        s, r, c = i // (CL * CL), (i // CL) % CL, i % CL
        where, found = jnp.int32(0), jnp.int32(0)
        for b in range(RUN):
            hit = (brow[s * RUN + b] % CL == r) & (bcol[s * RUN + b] % CL == c)
            where = jnp.where(hit, b, where)
            found = jnp.where(hit, 1, found)
        one = blk[s * RUN + where]
        one = jnp.where(found > 0, one, jnp.zeros_like(one))
        dense[s, pl.ds(pl.multiple_of(r * BS, BS), BS), pl.ds(pl.multiple_of(c * PAD, PAD), BS)] = one

    fetch.wait()

    owner_x = [owner[s] % X for s in range(STEPS)]
    owner_z = [owner[s] // X for s in range(STEPS)]
    far = jnp.maximum(z, Z - 1 - z)

    def pick(s, values):
        return jnp.where(s == 0, values[0], values[1])

    reach = LEAD + SKEW * far

    @pl.loop(0, LEAD + SKEW * (Z - 1) + T + LAG)
    def _(slot):
        @pl.when(slot < PIECES)
        def _():
            rows, first, second, half = piece(slot)
            drain(tr.at[half], r_tr.at[slot])
            send(tr.at[half], got.at[2, first], s_rl.at[0], r_fr.at[slot], right)
            drain(tl.at[half], r_tl.at[slot])
            send(tl.at[half], got.at[2, second], s_rl.at[1], r_fl.at[slot], left)

        @pl.when(slot < PIECES - AHEAD)
        def _():
            offer(slot + AHEAD)

        tg = slot - LEAD
        @pl.when((tg >= 0) & (tg < PIECES))
        def _():
            rows, first, second, half = piece(tg)
            drain(got.at[3, rows], r_right.at[tg])
            drain(got.at[1, rows], r_left.at[tg])
            drain(got.at[2, first], r_fr.at[tg])
            drain(got.at[2, second], r_fl.at[tg])

        def stream(t, inn, outt, rsem, ssem, has_in, has_out, dev):
            s, k = t // CHUNKS, t % CHUNKS
            rows = pl.ds(pl.multiple_of(k * CH, CH), CH)
            gap = (pick(s, owner_x) + X - x) % X
            own = got[0, rows]
            for d in range(1, X):
                own = jnp.where(gap == d, got[d, rows], own)

            @pl.when(has_in)
            def _():
                drain(inn.at[s, rows], rsem.at[t])
                outt[s, rows] = jnp.where(pick(s, owner_z) == z, own, inn[s, rows])

            @pl.when(jnp.logical_not(has_in))
            def _():
                outt[s, rows] = own

            @pl.when(has_out)
            def _():
                send(outt.at[s, rows], inn.at[s, rows], ssem, rsem.at[t], dev)

        tu = slot - LEAD - SKEW * z
        @pl.when((tu >= 0) & (tu < T))
        def _():
            stream(tu, up_in, up_out, r_up, s_z.at[0], z > 0, z < Z - 1, above)

        td = slot - LEAD - SKEW * (Z - 1 - z)
        @pl.when((td >= 0) & (td < T))
        def _():
            stream(td, dn_in, dn_out, r_dn, s_z.at[1], z < Z - 1, z > 0, below)

        tq = slot - reach
        @pl.when((tq >= 0) & (tq < T))
        def _():
            s, k = tq // CHUNKS, tq % CHUNKS
            rows = pl.ds(pl.multiple_of(k * CH, CH), CH)
            pan[s, x, rows] = jnp.where(pick(s, owner_z) <= z, up_out[s, rows], dn_out[s, rows])

            send(pan.at[s, x, rows], pan.at[s, x, rows], s_ag.at[0], r_ar.at[tq], right)
            send(pan.at[s, x, rows], pan.at[s, x, rows], s_ag.at[1], r_al.at[tq], left)

        tf = slot - reach - LAG
        @pl.when((tf >= 0) & (tf < T))
        def _():
            s = tf // PIECES
            rows, first, second, half = piece(tf % PIECES)
            drain(pan.at[s, xl, rows], r_ar.at[tf])
            send(pan.at[s, xl, first], pan.at[s, xl, first], s_fw.at[0], r_br.at[tf], right)
            drain(pan.at[s, xr, rows], r_al.at[tf])
            send(pan.at[s, xr, second], pan.at[s, xr, second], s_fw.at[1], r_bl.at[tf], left)

        @pl.when(slot < CL * CL)
        def _():
            turn(slot)

        @pl.when(slot < STEPS * CL * CL)
        def _():
            place(slot)

    def wait_panel(s):
        for k in range(PIECES):
            drain(pan.at[s, xo, k * PC : k * PC + PH], r_br.at[s * PIECES + k])
            drain(pan.at[s, xo, k * PC + PH : (k + 1) * PC], r_bl.at[s * PIECES + k])

    def panel_rows(s, n):
        lanes = slice(n * 256, (n + 1) * 256)
        rows = jnp.dot(
            dense[s], pan[s].reshape(CL * PAD, MODES)[:, lanes], preferred_element_type=F32
        ).astype(BF)
        for r in range(CL):
            tsp[s, r * PAD : r * PAD + BS, lanes] = rows[r * BS : (r + 1) * BS]

    def project(s, n):
        part = jnp.dot(
            basis_t[...], tsp[s, :, n * 256 : (n + 1) * 256], preferred_element_type=F32
        ).reshape(COLS, CORES, 8, 256)
        for k in range(CORES):
            share[k, s, n] = part[:, k]
        send(share.at[1 - core, s, n], core_in.at[s, n], s_core.at[s, n], r_core.at[s, n], at(core=1 - core))

    def over_plane(s):
        for n in range(NH):
            drain(core_in.at[s, n], r_core.at[s, n])
            for i in range(X):
                both = jnp.concatenate(
                    [share[core, s, n, zz * X + i] + core_in[s, n, zz * X + i] for zz in range(Z)], axis=0
                ).astype(BF)
                for j in range(2):
                    mine[s, i, n * 2 + j] = both[:, j * 128 : (j + 1) * 128]
        for i, (dx, dy) in enumerate(plane):
            xx, yy = (x + dx) % X, (y + dy) % Y
            send(mine.at[s, xx, yy], theirs.at[s, x, y], s_p.at[s, i], r_p.at[s, x * Y + y], at(x=xx, y=yy))

    def over_z():
        for s in range(STEPS):
            total = mine[s, x, y].astype(F32)
            for dx, dy in plane:
                xx, yy = (x + dx) % X, (y + dy) % Y
                drain(theirs.at[s, xx, yy], r_p.at[s, xx * Y + yy])
                total += theirs[s, xx, yy].astype(F32)
            for zz in range(Z):
                b3[s, zz] = total[zz * 8 : (zz + 1) * 8]
        for d in range(1, RING):
            p = (zg + d) % RING
            send(b3.at[p // Z, p % Z], z_in.at[zg], s_zz.at[d - 1], r_zz.at[zg], ring(d))
        z_in[zg] = b3[zh, z]

    def spread():
        for d in range(1, RING):
            p = (zg + d) % RING
            drain(z_in.at[p], r_zz.at[p])
        total = z_in[0]
        for p in range(1, RING):
            total += z_in[p]
        out_all[zh, y, core] = total
        for i, (dh, dy, dc) in enumerate(copies):
            hh, yy, cc = copy_at(dh, dy, dc)
            send(
                out_all.at[zh, y, core], out_all.at[zh, y, core], s_out.at[i],
                r_out.at[(zh * Y + y) * CORES + core], at(zh=hh, y=yy, core=cc),
            )

    def finish():
        for dh, dy, dc in copies:
            hh, yy, cc = copy_at(dh, dy, dc)
            drain(out_all.at[hh, yy, cc], r_out.at[(hh * Y + yy) * CORES + cc])
        for s in range(STEPS):
            for k in range(CORES):
                for j in range(Y):
                    out[s, k * 8 : (k + 1) * 8, j * 128 : (j + 1) * 128] = out_all[s, j, k]

    wait_panel(0)
    panel_rows(0, 0)
    panel_rows(0, 1)
    project(0, 0)
    project(0, 1)
    wait_panel(1)
    panel_rows(1, 0)
    over_plane(0)
    panel_rows(1, 1)
    project(1, 0)
    project(1, 1)
    over_plane(1)
    over_z()
    spread()
    finish()

    drain(basis.at[xr], s_x.at[0])
    drain(basis.at[xl], s_x.at[1])
    drain(tr, s_tr.at[0])
    drain(tl, s_tr.at[1])
    drain(tr, s_rl.at[0])
    drain(tl, s_rl.at[1])

    @pl.when(z < Z - 1)
    def _():
        drain(up_out, s_z.at[0])

    @pl.when(z > 0)
    def _():
        drain(dn_out, s_z.at[1])

    for i in range(2):
        drain(up_out, s_ag.at[i])
        drain(up_out.at[0], s_fw.at[i])
    for s in range(STEPS):
        for n in range(NH):
            drain(core_in.at[s, n], s_core.at[s, n])
        for i in range(len(plane)):
            drain(mine.at[s, 0, 0], s_p.at[s, i])
    for d in range(RING - 1):
        drain(z_in.at[0], s_zz.at[d])
    for i in range(len(copies)):
        drain(z_in.at[0], s_out.at[i])


def local(blocks, block_row, block_col, panel_owner, basis):
    dma = pltpu.SemaphoreType.DMA
    vmem = pltpu.VMEM
    scratch = [
        vmem((STEPS * RUN, BS, BS), BF),
        vmem((STEPS, CL * BS, CL * PAD), BF),
        vmem((MODES, CL * PAD), BF),
        vmem((STEPS, CL * PAD, MODES), BF),
        vmem((X, BS, MODES), BF),
        vmem((BS // 2, MODES), BF),
        vmem((BS // 2, MODES), BF),
        vmem((STEPS, BS, MODES), BF),
        vmem((STEPS, BS, MODES), BF),
        vmem((STEPS, BS, MODES), BF),
        vmem((STEPS, BS, MODES), BF),
        vmem((STEPS, CL, PAD, MODES), BF),
        vmem((CORES, STEPS, NH, COLS, 8, 256), F32),
        vmem((STEPS, NH, COLS, 8, 256), F32),
        vmem((STEPS, X, Y, 8 * Z, 128), BF),
        vmem((STEPS, X, Y, 8 * Z, 128), BF),
        vmem((STEPS, Z, 8, 128), F32),
        vmem((RING, 8, 128), F32),
        vmem((STEPS, Y, CORES, 8, 128), F32),
        dma, dma((2,)), dma((2,)), dma((2,)), dma((2,)), dma((2,)), dma((2,)),
        dma((STEPS, NH)), dma((STEPS, X * Y - 1)), dma((RING - 1,)), dma((ZH * Y * CORES - 1,)),
        dma((PIECES,)), dma((PIECES,)), dma((PIECES,)), dma((PIECES,)), dma((PIECES,)), dma((PIECES,)),
        dma((T,)), dma((T,)), dma((G,)), dma((G,)), dma((G,)), dma((G,)),
        dma((STEPS, NH)), dma((STEPS, X * Y)), dma((RING,)), dma((ZH * Y * CORES,)),
    ]
    smem = pl.BlockSpec(memory_space=pltpu.SMEM)
    whole = pl.BlockSpec(memory_space=pltpu.VMEM)
    result = pl.pallas_call(
        body,
        out_shape=jax.ShapeDtypeStruct((STEPS, CORES * 8, MODES), F32),
        in_specs=[smem, smem, smem, whole, pl.BlockSpec(memory_space=pl.ANY)],
        out_specs=whole,
        scratch_shapes=scratch,
        compiler_params=pltpu.CompilerParams(
            collective_id=0, has_side_effects=True, vmem_limit_bytes=56 * 1024 * 1024
        ),
        cost_estimate=pl.CostEstimate(flops=4_000_000_000, bytes_accessed=5_000_000, transcendentals=0),
        name="galerkin",
    )(panel_owner, block_row, block_col, basis, blocks)
    return jnp.transpose(result, (1, 0, 2))


def solution(mesh):
    return jax.shard_map(
        local,
        mesh=mesh,
        in_specs=(
            P(("grp", "col"), None, None),
            P(("grp", "col")),
            P(("grp", "col")),
            P(),
            P(("grp", "col"), None, None),
        ),
        out_specs=P("col", None, None),
        check_vma=False,
    )
```

```python
import jax
import jax.numpy as jnp
from jax import lax
from jax.experimental import pallas as pl
from jax.experimental.pallas import tpu as pltpu
from jax.sharding import PartitionSpec as P

X, Y, Z, ZH, CORES = 4, 4, 8, 2, 2
RING = Z * ZH
BS, MODES, STEPS, CL, RUN = 320, 512, 2, 4, 8
PAD = 384
W2 = STEPS * BS
CHUNKS = 10
CH = BS // CHUNKS
PIECES = 10
PC = BS // PIECES
PH = PC // 2
T = STEPS * CHUNKS
G = STEPS * PIECES
SKEW = 3
AHEAD = 4
LEAD = 3
WP = 8
WR = MODES // WP
HM = MODES // CORES
W_AT = 8
W_GO, W_STEP = 11, 2
W_SUM = 36
COLS = X * Z
NH = 2
BF, F32 = jnp.bfloat16, jnp.float32


class Here:
    def __init__(self):
        grp, col = lax.axis_index("grp"), lax.axis_index("col")
        self.core, self.y, self.zh = grp % CORES, (grp // CORES) % Y, grp // (CORES * Y)
        self.z, self.x = col // X, col % X
        self.zg = self.zh * Z + self.z

    def at(self, zh=None, y=None, core=None, z=None, x=None):
        zh = self.zh if zh is None else zh
        y = self.y if y is None else y
        core = self.core if core is None else core
        z = self.z if z is None else z
        x = self.x if x is None else x
        return ((zh * Y + y) * CORES + core, z * X + x)

    def ring(self, d):
        p = (self.zg + d) % RING
        return self.at(zh=p // Z, z=p % Z)


def send(src, dst, ssem, rsem, dev):
    pltpu.make_async_remote_copy(
        src_ref=src, dst_ref=dst, send_sem=ssem, recv_sem=rsem,
        device_id=dev, device_id_type=pl.DeviceIdType.MESH,
    ).start()


def drain(ref, sem):
    pltpu.make_async_copy(ref, ref, sem).wait()


def meet(peers):
    barrier = pltpu.get_barrier_semaphore()
    for dev in peers:
        pl.semaphore_signal(barrier, inc=1, device_id=dev, device_id_type=pl.DeviceIdType.MESH)
    pl.semaphore_wait(barrier, len(peers))


def body(
    owner, brow, bcol, basis, blocks, out,
    blk, dense, basis_t, w_own, w_out, w_in, w_sum, w_pass,
    got, tr, tl, up_in, dn_in, up_out, dn_out, q,
    mine, kept, theirs, b3, z_in, out_all,
    blk_sem, s_x, s_tr, s_rl, s_z, s_w, s_c, s_q, s_p, s_zz, s_out,
    r_right, r_left, r_tr, r_tl, r_fr, r_fl, r_up, r_dn, r_w, r_c, r_q, r_p, r_zz, r_out,
):
    here = Here()
    core, x, y, z, zh, zg, at, ring = here.core, here.x, here.y, here.z, here.zh, here.zg, here.at, here.ring
    xr, xl, xo = (x + 1) % X, (x + 3) % X, (x + 2) % X
    right, left, other = at(x=xr), at(x=xl), at(core=1 - core)
    above, below = at(z=(z + 1) % Z), at(z=(z + Z - 1) % Z)
    plane = [(dx, dy) for dx in range(X) for dy in range(Y) if dx or dy]
    copies = [(dh, dy, dc) for dh in range(ZH) for dy in range(Y) for dc in range(CORES) if dh or dy or dc]

    fetch = pltpu.make_async_copy(blocks, blk, blk_sem)
    fetch.start()

    def copy_at(dh, dy, dc):
        return (zh + dh) % ZH, (y + dy) % Y, (core + dc) % CORES

    peers = [at(x=(x + dx) % X, y=(y + dy) % Y) for dx, dy in plane]
    peers += [ring(d) for d in range(1, RING)]
    for dh, dy, dc in copies:
        if dc or (dh and dy):
            hh, yy, cc = copy_at(dh, dy, dc)
            peers.append(at(zh=hh, y=yy, core=cc))
    meet(peers)

    def piece(k):
        start = k * PC
        return (
            pl.ds(pl.multiple_of(start, PC), PC),
            pl.ds(pl.multiple_of(start, PH), PH),
            pl.ds(pl.multiple_of(start + PH, PH), PH),
            pl.ds(pl.multiple_of(k * PH, PH), PH),
        )

    def offer(k):
        rows, first, second, half = piece(k)
        send(basis.at[xo, first], tr.at[half], s_tr.at[0], r_tr.at[k], right)
        send(basis.at[xo, second], tl.at[half], s_tr.at[1], r_tl.at[k], left)
        send(basis.at[xr, rows], got.at[3, rows], s_x.at[0], r_right.at[k], right)
        send(basis.at[xl, rows], got.at[1, rows], s_x.at[1], r_left.at[k], left)

    for k in range(AHEAD):
        offer(k)
    got[0] = basis[x]
    for g in range(CORES):
        q[g, 0, BS:] = jnp.zeros((PAD - BS, MODES), BF)
        q[g, 1, : PAD - BS] = jnp.zeros((PAD - BS, MODES), BF)

    def turn(m):
        lanes = pl.ds(pl.multiple_of(m * 128, 128), 128)
        flipped = basis[:, :, lanes].reshape(CL * BS, 128).astype(F32).T.reshape(8, CORES, 8, CL * BS)
        for k in range(CORES):
            rows = pl.ds(pl.multiple_of(k * HM + m * 64, 64), 64)
            basis_t[rows] = flipped[:, k].reshape(64, CL * BS).astype(BF)

    def place(s, r, c):
        where, found = jnp.int32(0), jnp.int32(0)
        for b in range(RUN):
            hit = (brow[s * RUN + b] % CL == r) & (bcol[s * RUN + b] % CL == c)
            where = jnp.where(hit, b, where)
            found = jnp.where(hit, 1, found)
        one = blk[s * RUN + where]
        one = jnp.where(found > 0, one, jnp.zeros_like(one))
        dense[c, pl.ds(pl.multiple_of(r * BS, BS), BS), s * BS : (s + 1) * BS] = one

    def multiply(c):
        return jnp.dot(basis_t[...], dense[c], preferred_element_type=F32)

    fetch.wait()

    owner_x = [owner[s] % X for s in range(STEPS)]
    owner_z = [owner[s] // X for s in range(STEPS)]
    far = jnp.maximum(z, Z - 1 - z)

    def pick(s, values):
        return jnp.where(s == 0, values[0], values[1])

    reach = LEAD + SKEW * far

    @pl.loop(0, LEAD + SKEW * (Z - 1) + T)
    def _(slot):
        @pl.when(slot < PIECES)
        def _():
            rows, first, second, half = piece(slot)
            drain(tr.at[half], r_tr.at[slot])
            send(tr.at[half], got.at[2, first], s_rl.at[0], r_fr.at[slot], right)
            drain(tl.at[half], r_tl.at[slot])
            send(tl.at[half], got.at[2, second], s_rl.at[1], r_fl.at[slot], left)

        @pl.when(slot < PIECES - AHEAD)
        def _():
            offer(slot + AHEAD)

        tg = slot - LEAD
        @pl.when((tg >= 0) & (tg < PIECES))
        def _():
            rows, first, second, half = piece(tg)
            drain(got.at[3, rows], r_right.at[tg])
            drain(got.at[1, rows], r_left.at[tg])
            drain(got.at[2, first], r_fr.at[tg])
            drain(got.at[2, second], r_fl.at[tg])

        def stream(t, inn, outt, rsem, ssem, has_in, has_out, dev):
            s, k = t // CHUNKS, t % CHUNKS
            rows = pl.ds(pl.multiple_of(k * CH, CH), CH)
            gap = (pick(s, owner_x) + X - x) % X
            own = got[0, rows]
            for d in range(1, X):
                own = jnp.where(gap == d, got[d, rows], own)

            @pl.when(has_in)
            def _():
                drain(inn.at[s, rows], rsem.at[t])
                outt[s, rows] = jnp.where(pick(s, owner_z) == z, own, inn[s, rows])

            @pl.when(jnp.logical_not(has_in))
            def _():
                outt[s, rows] = own

            @pl.when(has_out)
            def _():
                send(outt.at[s, rows], inn.at[s, rows], ssem, rsem.at[t], dev)

        tu = slot - LEAD - SKEW * z
        @pl.when((tu >= 0) & (tu < T))
        def _():
            stream(tu, up_in, up_out, r_up, s_z.at[0], z > 0, z < Z - 1, above)

        td = slot - LEAD - SKEW * (Z - 1 - z)
        @pl.when((td >= 0) & (td < T))
        def _():
            stream(td, dn_in, dn_out, r_dn, s_z.at[1], z < Z - 1, z > 0, below)

        tq = slot - reach
        @pl.when((tq >= 0) & (tq < T))
        def _():
            s, k = tq // CHUNKS, tq % CHUNKS
            rows = pl.ds(pl.multiple_of(k * CH, CH), CH)
            here_rows = pl.ds(pl.multiple_of(s * (PAD - BS) + k * CH, CH), CH)
            q[core, s, here_rows] = jnp.where(pick(s, owner_z) <= z, up_out[s, rows], dn_out[s, rows])


            send(q.at[core, s, here_rows], q.at[core, s, here_rows], s_q, r_q.at[s], other)

        tw = slot - W_GO
        @pl.when((tw >= 0) & (tw % W_STEP == 0) & (tw < WP * W_STEP))
        def _():
            rows = pl.ds(pl.multiple_of(tw // W_STEP * WR, WR), WR)
            for d, dev in ((2, at(x=xo)), (1, right), (3, left)):
                send(w_out.at[d - 1, rows], w_in.at[d - 1, rows], s_w.at[d - 1], r_w.at[d - 1], dev)

        @pl.when(slot < 4)
        def _():
            turn(slot)

        @pl.when(slot < 8)
        def _():
            for i in range(2):
                for s in range(STEPS):
                    place(s, slot % CL, slot // CL * 2 + i)

        for i, d in enumerate((2, 1, 3)):
            @pl.when(slot == W_AT + i)
            def _(d=d):
                w_out[d - 1] = multiply((x + d) % X).astype(BF)

        @pl.when(slot == W_AT + 3)
        def _():
            w_own[...] = multiply(x)

        @pl.when(slot == W_SUM)
        def _():
            for d in range(X - 1):
                drain(w_in.at[d], r_w.at[d])

            @pl.loop(0, HM // 64)
            def _(m):
                for k in range(CORES):
                    rows = pl.ds(pl.multiple_of(k * HM + m * 64, 64), 64)
                    to = pl.ds(pl.multiple_of(m * 64, 64), 64)
                    total = w_own[rows]
                    for d in range(X - 1):
                        total += w_in[d, rows].astype(F32)
                    big = total.astype(BF)
                    small = (total - big.astype(F32)).astype(BF)

                    @pl.when(core == k)
                    def _():
                        w_sum[core, 0, to] = big
                        w_sum[core, 1, to] = small

                    @pl.when(core != k)
                    def _():
                        w_pass[0, to] = big
                        w_pass[1, to] = small

            send(w_pass, w_sum.at[core], s_c, r_c, other)

    def project(s, n):
        cols = slice(s * 256, s * 256 + PAD)
        part = jnp.zeros((HM, 256), F32)
        for g in range(CORES):
            panel = q[g, s, :, n * 256 : (n + 1) * 256]
            for t in range(2):
                part += jnp.dot(w_sum[g, t, :, cols], panel, preferred_element_type=F32)
        part = part.reshape(COLS, 8, 256)
        for i in range(X):
            both = jnp.concatenate([part[zz * X + i] for zz in range(Z)], axis=0)

            @pl.when(i == x)
            def _():
                for j in range(2):
                    kept[s, n * 2 + j] = both[:, j * 128 : (j + 1) * 128]

            both = both.astype(BF)
            for j in range(2):
                mine[s, i, n * 2 + j] = both[:, j * 128 : (j + 1) * 128]

    def over_plane(s):
        for i, (dx, dy) in enumerate(plane):
            xx, yy = (x + dx) % X, (y + dy) % Y
            send(mine.at[s, xx, yy], theirs.at[s, x, y], s_p.at[s, i], r_p.at[s, x * Y + y], at(x=xx, y=yy))

    def over_z():
        for s in range(STEPS):
            total = kept[s, y]
            for dx, dy in plane:
                xx, yy = (x + dx) % X, (y + dy) % Y
                drain(theirs.at[s, xx, yy], r_p.at[s, xx * Y + yy])
                total += theirs[s, xx, yy].astype(F32)
            for zz in range(Z):
                b3[s, zz] = total[zz * 8 : (zz + 1) * 8]
        for d in range(1, RING):
            p = (zg + d) % RING
            send(b3.at[p // Z, p % Z], z_in.at[zg], s_zz.at[d - 1], r_zz.at[zg], ring(d))
        z_in[zg] = b3[zh, z]

    def spread():
        for d in range(1, RING):
            p = (zg + d) % RING
            drain(z_in.at[p], r_zz.at[p])
        total = z_in[0]
        for p in range(1, RING):
            total += z_in[p]
        out_all[zh, y, core] = total
        for i, (dh, dy, dc) in enumerate(copies):
            hh, yy, cc = copy_at(dh, dy, dc)
            send(
                out_all.at[zh, y, core], out_all.at[zh, y, core], s_out.at[i],
                r_out.at[(zh * Y + y) * CORES + core], at(zh=hh, y=yy, core=cc),
            )

    def finish():
        for dh, dy, dc in copies:
            hh, yy, cc = copy_at(dh, dy, dc)
            drain(out_all.at[hh, yy, cc], r_out.at[(hh * Y + yy) * CORES + cc])
        for s in range(STEPS):
            for k in range(CORES):
                for j in range(Y):
                    out[s, k * 8 : (k + 1) * 8, j * 128 : (j + 1) * 128] = out_all[s, j, k]

    drain(w_sum.at[0], r_c)
    for s in range(STEPS):
        drain(up_in.at[s], r_q.at[s])
        for n in range(NH):
            project(s, n)
        over_plane(s)
    over_z()
    spread()
    finish()

    drain(basis.at[xr], s_x.at[0])
    drain(basis.at[xl], s_x.at[1])
    drain(tr, s_tr.at[0])
    drain(tl, s_tr.at[1])
    drain(tr, s_rl.at[0])
    drain(tl, s_rl.at[1])

    @pl.when(z < Z - 1)
    def _():
        drain(up_out, s_z.at[0])

    @pl.when(z > 0)
    def _():
        drain(dn_out, s_z.at[1])

    for d in range(X - 1):
        drain(w_out.at[d], s_w.at[d])
    drain(w_pass, s_c)
    drain(up_in, s_q)
    for s in range(STEPS):
        for i in range(len(plane)):
            drain(mine.at[s, 0, 0], s_p.at[s, i])
    for d in range(RING - 1):
        drain(z_in.at[0], s_zz.at[d])
    for i in range(len(copies)):
        drain(z_in.at[0], s_out.at[i])


def local(blocks, block_row, block_col, panel_owner, basis):
    dma = pltpu.SemaphoreType.DMA
    vmem = pltpu.VMEM
    scratch = [
        vmem((STEPS * RUN, BS, BS), BF),
        vmem((CL, CL * BS, W2), BF),
        vmem((MODES, CL * BS), BF),
        vmem((MODES, W2), F32),
        vmem((X - 1, MODES, W2), BF),
        vmem((X - 1, MODES, W2), BF),
        vmem((CORES, 2, HM, W2), BF),
        vmem((2, HM, W2), BF),
        vmem((X, BS, MODES), BF),
        vmem((BS // 2, MODES), BF),
        vmem((BS // 2, MODES), BF),
        vmem((STEPS, BS, MODES), BF),
        vmem((STEPS, BS, MODES), BF),
        vmem((STEPS, BS, MODES), BF),
        vmem((STEPS, BS, MODES), BF),
        vmem((CORES, STEPS, PAD, MODES), BF),
        vmem((STEPS, X, Y, 8 * Z, 128), BF),
        vmem((STEPS, Y, 8 * Z, 128), F32),
        vmem((STEPS, X, Y, 8 * Z, 128), BF),
        vmem((STEPS, Z, 8, 128), F32),
        vmem((RING, 8, 128), F32),
        vmem((STEPS, Y, CORES, 8, 128), F32),
        dma, dma((2,)), dma((2,)), dma((2,)), dma((2,)), dma((X - 1,)), dma, dma,
        dma((STEPS, X * Y - 1)), dma((RING - 1,)), dma((ZH * Y * CORES - 1,)),
        dma((PIECES,)), dma((PIECES,)), dma((PIECES,)), dma((PIECES,)), dma((PIECES,)), dma((PIECES,)),
        dma((T,)), dma((T,)), dma((X - 1,)), dma, dma((STEPS,)), dma((STEPS, X * Y)), dma((RING,)), dma((ZH * Y * CORES,)),
    ]
    smem = pl.BlockSpec(memory_space=pltpu.SMEM)
    whole = pl.BlockSpec(memory_space=pltpu.VMEM)
    result = pl.pallas_call(
        body,
        out_shape=jax.ShapeDtypeStruct((STEPS, CORES * 8, MODES), F32),
        in_specs=[smem, smem, smem, whole, pl.BlockSpec(memory_space=pl.ANY)],
        out_specs=whole,
        scratch_shapes=scratch,
        compiler_params=pltpu.CompilerParams(
            collective_id=0, has_side_effects=True, vmem_limit_bytes=56 * 1024 * 1024
        ),
        cost_estimate=pl.CostEstimate(flops=4_000_000_000, bytes_accessed=5_000_000, transcendentals=0),
        name="galerkin",
    )(panel_owner, block_row, block_col, basis, blocks)
    return jnp.transpose(result, (1, 0, 2))


def solution(mesh):
    return jax.shard_map(
        local,
        mesh=mesh,
        in_specs=(
            P(("grp", "col"), None, None),
            P(("grp", "col")),
            P(("grp", "col")),
            P(),
            P(("grp", "col"), None, None),
        ),
        out_specs=P("col", None, None),
        check_vma=False,
    )
```

```python
import jax
import jax.numpy as jnp
from jax import lax
from jax.experimental import pallas as pl
from jax.experimental.pallas import tpu as pltpu
from jax.sharding import PartitionSpec as P

X, Y, Z, ZH, CORES = 4, 4, 8, 2, 2
RING = Z * ZH
BS, MODES, STEPS, CL, RUN = 320, 512, 2, 4, 8
PAD = 384
W2 = STEPS * BS
CHUNKS = 10
CH = BS // CHUNKS
PIECES = 10
PC = BS // PIECES
PH = PC // 2
T = STEPS * CHUNKS
G = STEPS * PIECES
SKEW = 5
AHEAD = 5
LEAD = 5
WP = 8
WR = MODES // WP
HM = MODES // CORES
W_AT = 8
W_GO, W_STEP = 11, 4
W_SUM = 50
COLS = X * Z
NH = 2
BF, F32 = jnp.bfloat16, jnp.float32


class Here:
    def __init__(self):
        grp, col = lax.axis_index("grp"), lax.axis_index("col")
        self.core, self.y, self.zh = grp % CORES, (grp // CORES) % Y, grp // (CORES * Y)
        self.z, self.x = col // X, col % X
        self.zg = self.zh * Z + self.z

    def at(self, zh=None, y=None, core=None, z=None, x=None):
        zh = self.zh if zh is None else zh
        y = self.y if y is None else y
        core = self.core if core is None else core
        z = self.z if z is None else z
        x = self.x if x is None else x
        return ((zh * Y + y) * CORES + core, z * X + x)

    def ring(self, d):
        p = (self.zg + d) % RING
        return self.at(zh=p // Z, z=p % Z)


def send(src, dst, ssem, rsem, dev):
    pltpu.make_async_remote_copy(
        src_ref=src, dst_ref=dst, send_sem=ssem, recv_sem=rsem,
        device_id=dev, device_id_type=pl.DeviceIdType.MESH,
    ).start()


def drain(ref, sem):
    pltpu.make_async_copy(ref, ref, sem).wait()


def meet(peers):
    barrier = pltpu.get_barrier_semaphore()
    for dev in peers:
        pl.semaphore_signal(barrier, inc=1, device_id=dev, device_id_type=pl.DeviceIdType.MESH)
    pl.semaphore_wait(barrier, len(peers))


def body(
    owner, brow, bcol, basis, blocks, out,
    blk, dense, basis_t, w_own, w_out, w_in, w_sum, w_pass,
    got, tr, tl, up_in, dn_in, up_out, dn_out, q,
    mine, kept, theirs, b3, z_in, out_all,
    blk_sem, s_x, s_tr, s_rl, s_z, s_w, s_c, s_q, s_p, s_zz, s_out,
    r_right, r_left, r_tr, r_tl, r_fr, r_fl, r_up, r_dn, r_w, r_c, r_q, r_p, r_zz, r_out,
):
    here = Here()
    core, x, y, z, zh, zg, at, ring = here.core, here.x, here.y, here.z, here.zh, here.zg, here.at, here.ring
    xr, xl, xo = (x + 1) % X, (x + 3) % X, (x + 2) % X
    right, left, other = at(x=xr), at(x=xl), at(core=1 - core)
    above, below = at(z=(z + 1) % Z), at(z=(z + Z - 1) % Z)
    plane = [(dx, dy) for dx in range(X) for dy in range(Y) if dx or dy]
    copies = [(dh, dy, dc) for dh in range(ZH) for dy in range(Y) for dc in range(CORES) if dh or dy or dc]

    fetch = pltpu.make_async_copy(blocks, blk, blk_sem)
    fetch.start()

    def copy_at(dh, dy, dc):
        return (zh + dh) % ZH, (y + dy) % Y, (core + dc) % CORES

    peers = [at(x=(x + dx) % X, y=(y + dy) % Y) for dx, dy in plane]
    peers += [ring(d) for d in range(1, RING)]
    for dh, dy, dc in copies:
        if dc or (dh and dy):
            hh, yy, cc = copy_at(dh, dy, dc)
            peers.append(at(zh=hh, y=yy, core=cc))
    meet(peers)

    def piece(k):
        start = k * PC
        return (
            pl.ds(pl.multiple_of(start, PC), PC),
            pl.ds(pl.multiple_of(start, PH), PH),
            pl.ds(pl.multiple_of(start + PH, PH), PH),
            pl.ds(pl.multiple_of(k * PH, PH), PH),
        )

    def offer(k):
        rows, first, second, half = piece(k)
        send(basis.at[xo, first], tr.at[half], s_tr.at[0], r_tr.at[k], right)
        send(basis.at[xo, second], tl.at[half], s_tr.at[1], r_tl.at[k], left)
        send(basis.at[xr, rows], got.at[3, rows], s_x.at[0], r_right.at[k], right)
        send(basis.at[xl, rows], got.at[1, rows], s_x.at[1], r_left.at[k], left)

    for k in range(AHEAD):
        offer(k)
    got[0] = basis[x]
    for g in range(CORES):
        q[g, 0, BS:] = jnp.zeros((PAD - BS, MODES), BF)
        q[g, 1, : PAD - BS] = jnp.zeros((PAD - BS, MODES), BF)

    def turn(m):
        lanes = pl.ds(pl.multiple_of(m * 128, 128), 128)
        flipped = basis[:, :, lanes].reshape(CL * BS, 128).astype(F32).T.reshape(8, CORES, 8, CL * BS)
        for k in range(CORES):
            rows = pl.ds(pl.multiple_of(k * HM + m * 64, 64), 64)
            basis_t[rows] = flipped[:, k].reshape(64, CL * BS).astype(BF)

    def place(s, r, c):
        where, found = jnp.int32(0), jnp.int32(0)
        for b in range(RUN):
            hit = (brow[s * RUN + b] % CL == r) & (bcol[s * RUN + b] % CL == c)
            where = jnp.where(hit, b, where)
            found = jnp.where(hit, 1, found)
        one = blk[s * RUN + where]
        one = jnp.where(found > 0, one, jnp.zeros_like(one))
        dense[c, pl.ds(pl.multiple_of(r * BS, BS), BS), s * BS : (s + 1) * BS] = one

    def multiply(c):
        return jnp.dot(basis_t[...], dense[c], preferred_element_type=F32)

    fetch.wait()

    owner_x = [owner[s] % X for s in range(STEPS)]
    owner_z = [owner[s] // X for s in range(STEPS)]
    far = jnp.maximum(z, Z - 1 - z)

    def pick(s, values):
        return jnp.where(s == 0, values[0], values[1])

    reach = LEAD + SKEW * far

    @pl.loop(0, LEAD + SKEW * (Z - 1) + T)
    def _(slot):
        @pl.when(slot < PIECES)
        def _():
            rows, first, second, half = piece(slot)
            drain(tr.at[half], r_tr.at[slot])
            send(tr.at[half], got.at[2, first], s_rl.at[0], r_fr.at[slot], right)
            drain(tl.at[half], r_tl.at[slot])
            send(tl.at[half], got.at[2, second], s_rl.at[1], r_fl.at[slot], left)

        @pl.when(slot < PIECES - AHEAD)
        def _():
            offer(slot + AHEAD)

        tg = slot - LEAD
        @pl.when((tg >= 0) & (tg < PIECES))
        def _():
            rows, first, second, half = piece(tg)
            drain(got.at[3, rows], r_right.at[tg])
            drain(got.at[1, rows], r_left.at[tg])
            drain(got.at[2, first], r_fr.at[tg])
            drain(got.at[2, second], r_fl.at[tg])

        def stream(t, inn, outt, rsem, ssem, has_in, has_out, dev):
            s, k = t // CHUNKS, t % CHUNKS
            rows = pl.ds(pl.multiple_of(k * CH, CH), CH)
            gap = (pick(s, owner_x) + X - x) % X
            own = got[0, rows]
            for d in range(1, X):
                own = jnp.where(gap == d, got[d, rows], own)

            @pl.when(has_in)
            def _():
                drain(inn.at[s, rows], rsem.at[t])
                outt[s, rows] = jnp.where(pick(s, owner_z) == z, own, inn[s, rows])

            @pl.when(jnp.logical_not(has_in))
            def _():
                outt[s, rows] = own

            @pl.when(has_out)
            def _():
                send(outt.at[s, rows], inn.at[s, rows], ssem, rsem.at[t], dev)

        tu = slot - LEAD - SKEW * z
        @pl.when((tu >= 0) & (tu < T))
        def _():
            stream(tu, up_in, up_out, r_up, s_z.at[0], z > 0, z < Z - 1, above)

        td = slot - LEAD - SKEW * (Z - 1 - z)
        @pl.when((td >= 0) & (td < T))
        def _():
            stream(td, dn_in, dn_out, r_dn, s_z.at[1], z < Z - 1, z > 0, below)

        tq = slot - reach
        @pl.when((tq >= 0) & (tq < T))
        def _():
            s, k = tq // CHUNKS, tq % CHUNKS
            rows = pl.ds(pl.multiple_of(k * CH, CH), CH)
            here_rows = pl.ds(pl.multiple_of(s * (PAD - BS) + k * CH, CH), CH)
            q[core, s, here_rows] = jnp.where(pick(s, owner_z) <= z, up_out[s, rows], dn_out[s, rows])


            send(q.at[core, s, here_rows], q.at[core, s, here_rows], s_q, r_q.at[s], other)

        tw = slot - W_GO
        @pl.when((tw >= 0) & (tw % W_STEP == 0) & (tw < WP * W_STEP))
        def _():
            rows = pl.ds(pl.multiple_of(tw // W_STEP * WR, WR), WR)
            for d, dev in ((2, at(x=xo)), (1, right), (3, left)):
                send(w_out.at[d - 1, rows], w_in.at[d - 1, rows], s_w.at[d - 1], r_w.at[d - 1], dev)

        @pl.when(slot < 4)
        def _():
            turn(slot)

        @pl.when(slot < 8)
        def _():
            for i in range(2):
                for s in range(STEPS):
                    place(s, slot % CL, slot // CL * 2 + i)

        for i, d in enumerate((2, 1, 3)):
            @pl.when(slot == W_AT + i)
            def _(d=d):
                w_out[d - 1] = multiply((x + d) % X).astype(BF)

        @pl.when(slot == W_AT + 3)
        def _():
            w_own[...] = multiply(x)

        @pl.when(slot == W_SUM)
        def _():
            for d in range(X - 1):
                drain(w_in.at[d], r_w.at[d])

        @pl.when((slot >= W_SUM) & (slot < W_SUM + HM // 64))
        def _():
            m = slot - W_SUM
            to = pl.ds(pl.multiple_of(m * 64, 64), 64)
            for k in range(CORES):
                rows = pl.ds(pl.multiple_of(k * HM + m * 64, 64), 64)
                total = w_own[rows]
                for d in range(X - 1):
                    total += w_in[d, rows].astype(F32)
                big = total.astype(BF)
                small = (total - big.astype(F32)).astype(BF)

                @pl.when(core == k)
                def _():
                    w_sum[core, 0, to] = big
                    w_sum[core, 1, to] = small

                @pl.when(core != k)
                def _():
                    w_pass[0, to] = big
                    w_pass[1, to] = small

        @pl.when(slot == W_SUM + HM // 64 - 1)
        def _():
            send(w_pass, w_sum.at[core], s_c, r_c, other)

    def project(s, n):
        cols = slice(s * 256, s * 256 + PAD)
        part = jnp.zeros((HM, 256), F32)
        for g in range(CORES):
            panel = q[g, s, :, n * 256 : (n + 1) * 256]
            for t in range(2):
                part += jnp.dot(w_sum[g, t, :, cols], panel, preferred_element_type=F32)
        part = part.reshape(COLS, 8, 256)
        for i in range(X):
            both = jnp.concatenate([part[zz * X + i] for zz in range(Z)], axis=0)

            @pl.when(i == x)
            def _():
                for j in range(2):
                    kept[s, n * 2 + j] = both[:, j * 128 : (j + 1) * 128]

            both = both.astype(BF)
            for j in range(2):
                mine[s, i, n * 2 + j] = both[:, j * 128 : (j + 1) * 128]

    def over_plane(s):
        for i, (dx, dy) in enumerate(plane):
            xx, yy = (x + dx) % X, (y + dy) % Y
            send(mine.at[s, xx, yy], theirs.at[s, x, y], s_p.at[s, i], r_p.at[s, x * Y + y], at(x=xx, y=yy))

    def over_z():
        for s in range(STEPS):
            total = kept[s, y]
            for dx, dy in plane:
                xx, yy = (x + dx) % X, (y + dy) % Y
                drain(theirs.at[s, xx, yy], r_p.at[s, xx * Y + yy])
                total += theirs[s, xx, yy].astype(F32)
            for zz in range(Z):
                b3[s, zz] = total[zz * 8 : (zz + 1) * 8]
        for d in range(1, RING):
            p = (zg + d) % RING
            send(b3.at[p // Z, p % Z], z_in.at[zg], s_zz.at[d - 1], r_zz.at[zg], ring(d))
        z_in[zg] = b3[zh, z]

    def spread():
        for d in range(1, RING):
            p = (zg + d) % RING
            drain(z_in.at[p], r_zz.at[p])
        total = z_in[0]
        for p in range(1, RING):
            total += z_in[p]
        out_all[zh, y, core] = total
        for i, (dh, dy, dc) in enumerate(copies):
            hh, yy, cc = copy_at(dh, dy, dc)
            send(
                out_all.at[zh, y, core], out_all.at[zh, y, core], s_out.at[i],
                r_out.at[(zh * Y + y) * CORES + core], at(zh=hh, y=yy, core=cc),
            )

    def finish():
        for dh, dy, dc in copies:
            hh, yy, cc = copy_at(dh, dy, dc)
            drain(out_all.at[hh, yy, cc], r_out.at[(hh * Y + yy) * CORES + cc])
        for s in range(STEPS):
            for k in range(CORES):
                for j in range(Y):
                    out[s, k * 8 : (k + 1) * 8, j * 128 : (j + 1) * 128] = out_all[s, j, k]

    drain(w_sum.at[0], r_c)
    for s in range(STEPS):
        drain(up_in.at[s], r_q.at[s])
        for n in range(NH):
            project(s, n)
        over_plane(s)
    over_z()
    spread()
    finish()

    drain(basis.at[xr], s_x.at[0])
    drain(basis.at[xl], s_x.at[1])
    drain(tr, s_tr.at[0])
    drain(tl, s_tr.at[1])
    drain(tr, s_rl.at[0])
    drain(tl, s_rl.at[1])

    @pl.when(z < Z - 1)
    def _():
        drain(up_out, s_z.at[0])

    @pl.when(z > 0)
    def _():
        drain(dn_out, s_z.at[1])

    for d in range(X - 1):
        drain(w_out.at[d], s_w.at[d])
    drain(w_pass, s_c)
    drain(up_in, s_q)
    for s in range(STEPS):
        for i in range(len(plane)):
            drain(mine.at[s, 0, 0], s_p.at[s, i])
    for d in range(RING - 1):
        drain(z_in.at[0], s_zz.at[d])
    for i in range(len(copies)):
        drain(z_in.at[0], s_out.at[i])


def local(blocks, block_row, block_col, panel_owner, basis):
    dma = pltpu.SemaphoreType.DMA
    vmem = pltpu.VMEM
    scratch = [
        vmem((STEPS * RUN, BS, BS), BF),
        vmem((CL, CL * BS, W2), BF),
        vmem((MODES, CL * BS), BF),
        vmem((MODES, W2), F32),
        vmem((X - 1, MODES, W2), BF),
        vmem((X - 1, MODES, W2), BF),
        vmem((CORES, 2, HM, W2), BF),
        vmem((2, HM, W2), BF),
        vmem((X, BS, MODES), BF),
        vmem((BS // 2, MODES), BF),
        vmem((BS // 2, MODES), BF),
        vmem((STEPS, BS, MODES), BF),
        vmem((STEPS, BS, MODES), BF),
        vmem((STEPS, BS, MODES), BF),
        vmem((STEPS, BS, MODES), BF),
        vmem((CORES, STEPS, PAD, MODES), BF),
        vmem((STEPS, X, Y, 8 * Z, 128), BF),
        vmem((STEPS, Y, 8 * Z, 128), F32),
        vmem((STEPS, X, Y, 8 * Z, 128), BF),
        vmem((STEPS, Z, 8, 128), F32),
        vmem((RING, 8, 128), F32),
        vmem((STEPS, Y, CORES, 8, 128), F32),
        dma, dma((2,)), dma((2,)), dma((2,)), dma((2,)), dma((X - 1,)), dma, dma,
        dma((STEPS, X * Y - 1)), dma((RING - 1,)), dma((ZH * Y * CORES - 1,)),
        dma((PIECES,)), dma((PIECES,)), dma((PIECES,)), dma((PIECES,)), dma((PIECES,)), dma((PIECES,)),
        dma((T,)), dma((T,)), dma((X - 1,)), dma, dma((STEPS,)), dma((STEPS, X * Y)), dma((RING,)), dma((ZH * Y * CORES,)),
    ]
    smem = pl.BlockSpec(memory_space=pltpu.SMEM)
    whole = pl.BlockSpec(memory_space=pltpu.VMEM)
    result = pl.pallas_call(
        body,
        out_shape=jax.ShapeDtypeStruct((STEPS, CORES * 8, MODES), F32),
        in_specs=[smem, smem, smem, whole, pl.BlockSpec(memory_space=pl.ANY)],
        out_specs=whole,
        scratch_shapes=scratch,
        compiler_params=pltpu.CompilerParams(
            collective_id=0, has_side_effects=True, vmem_limit_bytes=56 * 1024 * 1024
        ),
        cost_estimate=pl.CostEstimate(flops=4_000_000_000, bytes_accessed=5_000_000, transcendentals=0),
        name="galerkin",
    )(panel_owner, block_row, block_col, basis, blocks)
    return jnp.transpose(result, (1, 0, 2))


def solution(mesh):
    return jax.shard_map(
        local,
        mesh=mesh,
        in_specs=(
            P(("grp", "col"), None, None),
            P(("grp", "col")),
            P(("grp", "col")),
            P(),
            P(("grp", "col"), None, None),
        ),
        out_specs=P("col", None, None),
        check_vma=False,
    )
```

```python
import jax
import jax.numpy as jnp
from jax import lax
from jax.experimental import pallas as pl
from jax.experimental.pallas import tpu as pltpu
from jax.sharding import PartitionSpec as P

X, Y, Z, ZH, CORES = 4, 4, 8, 2, 2
RING = Z * ZH
BS, MODES, STEPS, CL, RUN = 320, 512, 2, 4, 8
PAD = 384
W2 = STEPS * BS
CHUNKS = 10
CH = BS // CHUNKS
PIECES = 10
PC = BS // PIECES
PH = PC // 2
T = STEPS * CHUNKS
G = STEPS * PIECES
SKEW = 5
AHEAD = 5
LEAD = 5
WP = 8
WR = MODES // WP
HM = MODES // CORES
W_AT = 8
W_GO, W_STEP = 11, 3
W_SUM = 46
EARLY = 56
COLS = X * Z
NH = 2
BF, F32 = jnp.bfloat16, jnp.float32


class Here:
    def __init__(self):
        grp, col = lax.axis_index("grp"), lax.axis_index("col")
        self.core, self.y, self.zh = grp % CORES, (grp // CORES) % Y, grp // (CORES * Y)
        self.z, self.x = col // X, col % X
        self.zg = self.zh * Z + self.z

    def at(self, zh=None, y=None, core=None, z=None, x=None):
        zh = self.zh if zh is None else zh
        y = self.y if y is None else y
        core = self.core if core is None else core
        z = self.z if z is None else z
        x = self.x if x is None else x
        return ((zh * Y + y) * CORES + core, z * X + x)

    def ring(self, d):
        p = (self.zg + d) % RING
        return self.at(zh=p // Z, z=p % Z)


def send(src, dst, ssem, rsem, dev):
    pltpu.make_async_remote_copy(
        src_ref=src, dst_ref=dst, send_sem=ssem, recv_sem=rsem,
        device_id=dev, device_id_type=pl.DeviceIdType.MESH,
    ).start()


def drain(ref, sem):
    pltpu.make_async_copy(ref, ref, sem).wait()


def greet(peers):
    barrier = pltpu.get_barrier_semaphore()
    for dev in peers:
        pl.semaphore_signal(barrier, inc=1, device_id=dev, device_id_type=pl.DeviceIdType.MESH)
    return barrier


def body(
    owner, brow, bcol, basis, blocks, out,
    blk, dense, basis_t, w_own, w_out, w_in, w_sum, w_pass,
    got, tr, tl, up_in, dn_in, up_out, dn_out, q,
    mine, kept, theirs, b3, z_in, out_all,
    blk_sem, s_x, s_tr, s_rl, s_z, s_w, s_c, s_q, s_p, s_zz, s_out,
    r_right, r_left, r_tr, r_tl, r_fr, r_fl, r_up, r_dn, r_w, r_c, r_q, r_p, r_zz, r_out,
):
    here = Here()
    core, x, y, z, zh, zg, at, ring = here.core, here.x, here.y, here.z, here.zh, here.zg, here.at, here.ring
    xr, xl, xo = (x + 1) % X, (x + 3) % X, (x + 2) % X
    right, left, other = at(x=xr), at(x=xl), at(core=1 - core)
    above, below = at(z=(z + 1) % Z), at(z=(z + Z - 1) % Z)
    plane = [(dx, dy) for dx in range(X) for dy in range(Y) if dx or dy]
    copies = [(dh, dy, dc) for dh in range(ZH) for dy in range(Y) for dc in range(CORES) if dh or dy or dc]

    fetch = pltpu.make_async_copy(blocks, blk, blk_sem)
    fetch.start()

    def copy_at(dh, dy, dc):
        return (zh + dh) % ZH, (y + dy) % Y, (core + dc) % CORES

    peers = [at(x=(x + dx) % X, y=(y + dy) % Y) for dx, dy in plane]
    peers += [ring(d) for d in range(1, RING)]
    for dh, dy, dc in copies:
        if dc or (dh and dy):
            hh, yy, cc = copy_at(dh, dy, dc)
            peers.append(at(zh=hh, y=yy, core=cc))
    barrier = greet(peers)
    got[0] = basis[x]
    for g in range(CORES):
        q[g, 0, BS:] = jnp.zeros((PAD - BS, MODES), BF)
        q[g, 1, : PAD - BS] = jnp.zeros((PAD - BS, MODES), BF)
    pl.semaphore_wait(barrier, len(peers))

    def piece(k):
        start = k * PC
        return (
            pl.ds(pl.multiple_of(start, PC), PC),
            pl.ds(pl.multiple_of(start, PH), PH),
            pl.ds(pl.multiple_of(start + PH, PH), PH),
            pl.ds(pl.multiple_of(k * PH, PH), PH),
        )

    def offer(k):
        rows, first, second, half = piece(k)
        send(basis.at[xo, first], tr.at[half], s_tr.at[0], r_tr.at[k], right)
        send(basis.at[xo, second], tl.at[half], s_tr.at[1], r_tl.at[k], left)
        send(basis.at[xr, rows], got.at[3, rows], s_x.at[0], r_right.at[k], right)
        send(basis.at[xl, rows], got.at[1, rows], s_x.at[1], r_left.at[k], left)

    for k in range(AHEAD):
        offer(k)
    def turn(m):
        lanes = pl.ds(pl.multiple_of(m * 128, 128), 128)
        flipped = basis[:, :, lanes].reshape(CL * BS, 128).astype(F32).T.reshape(8, CORES, 8, CL * BS)
        for k in range(CORES):
            rows = pl.ds(pl.multiple_of(k * HM + m * 64, 64), 64)
            basis_t[rows] = flipped[:, k].reshape(64, CL * BS).astype(BF)

    def place(s, r, c):
        where, found = jnp.int32(0), jnp.int32(0)
        for b in range(RUN):
            hit = (brow[s * RUN + b] % CL == r) & (bcol[s * RUN + b] % CL == c)
            where = jnp.where(hit, b, where)
            found = jnp.where(hit, 1, found)
        one = blk[s * RUN + where]
        one = jnp.where(found > 0, one, jnp.zeros_like(one))
        dense[c, pl.ds(pl.multiple_of(r * BS, BS), BS), s * BS : (s + 1) * BS] = one

    def multiply(c):
        return jnp.dot(basis_t[...], dense[c], preferred_element_type=F32)

    fetch.wait()

    def project(s, n):
        cols = slice(s * 256, s * 256 + PAD)
        part = jnp.zeros((HM, 256), F32)
        for g in range(CORES):
            panel = q[g, s, :, n * 256 : (n + 1) * 256]
            for t in range(2):
                part += jnp.dot(w_sum[g, t, :, cols], panel, preferred_element_type=F32)
        part = part.reshape(COLS, 8, 256)
        for i in range(X):
            both = jnp.concatenate([part[zz * X + i] for zz in range(Z)], axis=0)

            @pl.when(i == x)
            def _():
                for j in range(2):
                    kept[s, n * 2 + j] = both[:, j * 128 : (j + 1) * 128]

            both = both.astype(BF)
            for j in range(2):
                mine[s, i, n * 2 + j] = both[:, j * 128 : (j + 1) * 128]

    def over_plane(s):
        for i, (dx, dy) in enumerate(plane):
            xx, yy = (x + dx) % X, (y + dy) % Y
            send(mine.at[s, xx, yy], theirs.at[s, x, y], s_p.at[s, i], r_p.at[s, x * Y + y], at(x=xx, y=yy))

    owner_x = [owner[s] % X for s in range(STEPS)]
    owner_z = [owner[s] // X for s in range(STEPS)]
    far = jnp.maximum(z, Z - 1 - z)

    def pick(s, values):
        return jnp.where(s == 0, values[0], values[1])

    reach = LEAD + SKEW * far

    @pl.loop(0, LEAD + SKEW * (Z - 1) + T)
    def _(slot):
        @pl.when(slot < PIECES)
        def _():
            rows, first, second, half = piece(slot)
            drain(tr.at[half], r_tr.at[slot])
            send(tr.at[half], got.at[2, first], s_rl.at[0], r_fr.at[slot], right)
            drain(tl.at[half], r_tl.at[slot])
            send(tl.at[half], got.at[2, second], s_rl.at[1], r_fl.at[slot], left)

        @pl.when(slot < PIECES - AHEAD)
        def _():
            offer(slot + AHEAD)

        tg = slot - LEAD
        @pl.when((tg >= 0) & (tg < PIECES))
        def _():
            rows, first, second, half = piece(tg)
            drain(got.at[3, rows], r_right.at[tg])
            drain(got.at[1, rows], r_left.at[tg])
            drain(got.at[2, first], r_fr.at[tg])
            drain(got.at[2, second], r_fl.at[tg])

        def stream(t, inn, outt, rsem, ssem, has_in, has_out, dev):
            s, k = t // CHUNKS, t % CHUNKS
            rows = pl.ds(pl.multiple_of(k * CH, CH), CH)
            gap = (pick(s, owner_x) + X - x) % X
            own = got[0, rows]
            for d in range(1, X):
                own = jnp.where(gap == d, got[d, rows], own)

            @pl.when(has_in)
            def _():
                drain(inn.at[s, rows], rsem.at[t])
                outt[s, rows] = jnp.where(pick(s, owner_z) == z, own, inn[s, rows])

            @pl.when(jnp.logical_not(has_in))
            def _():
                outt[s, rows] = own

            @pl.when(has_out)
            def _():
                send(outt.at[s, rows], inn.at[s, rows], ssem, rsem.at[t], dev)

        tu = slot - LEAD - SKEW * z
        @pl.when((tu >= 0) & (tu < T))
        def _():
            stream(tu, up_in, up_out, r_up, s_z.at[0], z > 0, z < Z - 1, above)

        td = slot - LEAD - SKEW * (Z - 1 - z)
        @pl.when((td >= 0) & (td < T))
        def _():
            stream(td, dn_in, dn_out, r_dn, s_z.at[1], z < Z - 1, z > 0, below)

        tq = slot - reach
        @pl.when((tq >= 0) & (tq < T))
        def _():
            s, k = tq // CHUNKS, tq % CHUNKS
            rows = pl.ds(pl.multiple_of(k * CH, CH), CH)
            here_rows = pl.ds(pl.multiple_of(s * (PAD - BS) + k * CH, CH), CH)
            q[core, s, here_rows] = jnp.where(pick(s, owner_z) <= z, up_out[s, rows], dn_out[s, rows])


            send(q.at[core, s, here_rows], q.at[core, s, here_rows], s_q, r_q.at[s], other)

        tw = slot - W_GO
        @pl.when((tw >= 0) & (tw % W_STEP == 0) & (tw < WP * W_STEP))
        def _():
            rows = pl.ds(pl.multiple_of(tw // W_STEP * WR, WR), WR)
            for d, dev in ((2, at(x=xo)), (1, right), (3, left)):
                send(w_out.at[d - 1, rows], w_in.at[d - 1, rows], s_w.at[d - 1], r_w.at[d - 1], dev)

        @pl.when(slot < 4)
        def _():
            turn(slot)

        @pl.when(slot < 8)
        def _():
            for i in range(2):
                for s in range(STEPS):
                    place(s, slot % CL, slot // CL * 2 + i)

        for i, d in enumerate((2, 1, 3)):
            @pl.when(slot == W_AT + i)
            def _(d=d):
                w_out[d - 1] = multiply((x + d) % X).astype(BF)

        @pl.when(slot == W_AT + 3)
        def _():
            w_own[...] = multiply(x)

        @pl.when(slot == W_SUM)
        def _():
            for d in range(X - 1):
                drain(w_in.at[d], r_w.at[d])

        @pl.when((slot >= W_SUM) & (slot < W_SUM + HM // 64))
        def _():
            m = slot - W_SUM
            to = pl.ds(pl.multiple_of(m * 64, 64), 64)
            for k in range(CORES):
                rows = pl.ds(pl.multiple_of(k * HM + m * 64, 64), 64)
                total = w_own[rows]
                for d in range(X - 1):
                    total += w_in[d, rows].astype(F32)
                big = total.astype(BF)
                small = (total - big.astype(F32)).astype(BF)

                @pl.when(core == k)
                def _():
                    w_sum[core, 0, to] = big
                    w_sum[core, 1, to] = small

                @pl.when(core != k)
                def _():
                    w_pass[0, to] = big
                    w_pass[1, to] = small

        @pl.when(slot == W_SUM + HM // 64 - 1)
        def _():
            send(w_pass, w_sum.at[core], s_c, r_c, other)

        @pl.when(slot == EARLY)
        def _():
            drain(w_sum.at[0], r_c)
            drain(up_in.at[0], r_q.at[0])
            project(0, 0)

        @pl.when(slot == EARLY + 1)
        def _():
            project(0, 1)
            over_plane(0)

    def over_z():
        for s in range(STEPS):
            total = kept[s, y]
            for dx, dy in plane:
                xx, yy = (x + dx) % X, (y + dy) % Y
                drain(theirs.at[s, xx, yy], r_p.at[s, xx * Y + yy])
                total += theirs[s, xx, yy].astype(F32)
            for zz in range(Z):
                b3[s, zz] = total[zz * 8 : (zz + 1) * 8]
        for d in range(1, RING):
            p = (zg + d) % RING
            send(b3.at[p // Z, p % Z], z_in.at[zg], s_zz.at[d - 1], r_zz.at[zg], ring(d))
        z_in[zg] = b3[zh, z]

    def spread():
        for d in range(1, RING):
            p = (zg + d) % RING
            drain(z_in.at[p], r_zz.at[p])
        total = z_in[0]
        for p in range(1, RING):
            total += z_in[p]
        out_all[zh, y, core] = total
        for i, (dh, dy, dc) in enumerate(copies):
            hh, yy, cc = copy_at(dh, dy, dc)
            send(
                out_all.at[zh, y, core], out_all.at[zh, y, core], s_out.at[i],
                r_out.at[(zh * Y + y) * CORES + core], at(zh=hh, y=yy, core=cc),
            )

    def finish():
        for dh, dy, dc in copies:
            hh, yy, cc = copy_at(dh, dy, dc)
            drain(out_all.at[hh, yy, cc], r_out.at[(hh * Y + yy) * CORES + cc])
        for s in range(STEPS):
            for k in range(CORES):
                for j in range(Y):
                    out[s, k * 8 : (k + 1) * 8, j * 128 : (j + 1) * 128] = out_all[s, j, k]

    drain(up_in.at[1], r_q.at[1])
    project(1, 0)
    project(1, 1)
    over_plane(1)

    drain(basis.at[xr], s_x.at[0])
    drain(basis.at[xl], s_x.at[1])
    for i in range(2):
        drain(tr, s_tr.at[i])
        drain(tr, s_rl.at[i])

    @pl.when(z < Z - 1)
    def _():
        drain(up_out, s_z.at[0])

    @pl.when(z > 0)
    def _():
        drain(dn_out, s_z.at[1])

    for d in range(X - 1):
        drain(w_out.at[d], s_w.at[d])
    drain(w_pass, s_c)
    drain(up_in, s_q)

    over_z()
    for s in range(STEPS):
        for i in range(len(plane)):
            drain(mine.at[s, 0, 0], s_p.at[s, i])
    spread()
    for d in range(RING - 1):
        drain(z_in.at[0], s_zz.at[d])
    finish()
    for i in range(len(copies)):
        drain(z_in.at[0], s_out.at[i])


def local(blocks, block_row, block_col, panel_owner, basis):
    dma = pltpu.SemaphoreType.DMA
    vmem = pltpu.VMEM
    scratch = [
        vmem((STEPS * RUN, BS, BS), BF),
        vmem((CL, CL * BS, W2), BF),
        vmem((MODES, CL * BS), BF),
        vmem((MODES, W2), F32),
        vmem((X - 1, MODES, W2), BF),
        vmem((X - 1, MODES, W2), BF),
        vmem((CORES, 2, HM, W2), BF),
        vmem((2, HM, W2), BF),
        vmem((X, BS, MODES), BF),
        vmem((BS // 2, MODES), BF),
        vmem((BS // 2, MODES), BF),
        vmem((STEPS, BS, MODES), BF),
        vmem((STEPS, BS, MODES), BF),
        vmem((STEPS, BS, MODES), BF),
        vmem((STEPS, BS, MODES), BF),
        vmem((CORES, STEPS, PAD, MODES), BF),
        vmem((STEPS, X, Y, 8 * Z, 128), BF),
        vmem((STEPS, Y, 8 * Z, 128), F32),
        vmem((STEPS, X, Y, 8 * Z, 128), BF),
        vmem((STEPS, Z, 8, 128), F32),
        vmem((RING, 8, 128), F32),
        vmem((STEPS, Y, CORES, 8, 128), F32),
        dma, dma((2,)), dma((2,)), dma((2,)), dma((2,)), dma((X - 1,)), dma, dma,
        dma((STEPS, X * Y - 1)), dma((RING - 1,)), dma((ZH * Y * CORES - 1,)),
        dma((PIECES,)), dma((PIECES,)), dma((PIECES,)), dma((PIECES,)), dma((PIECES,)), dma((PIECES,)),
        dma((T,)), dma((T,)), dma((X - 1,)), dma, dma((STEPS,)), dma((STEPS, X * Y)), dma((RING,)), dma((ZH * Y * CORES,)),
    ]
    smem = pl.BlockSpec(memory_space=pltpu.SMEM)
    whole = pl.BlockSpec(memory_space=pltpu.VMEM)
    result = pl.pallas_call(
        body,
        out_shape=jax.ShapeDtypeStruct((STEPS, CORES * 8, MODES), F32),
        in_specs=[smem, smem, smem, whole, pl.BlockSpec(memory_space=pl.ANY)],
        out_specs=whole,
        scratch_shapes=scratch,
        compiler_params=pltpu.CompilerParams(
            collective_id=0, has_side_effects=True, vmem_limit_bytes=56 * 1024 * 1024
        ),
        cost_estimate=pl.CostEstimate(flops=4_000_000_000, bytes_accessed=5_000_000, transcendentals=0),
        name="galerkin",
    )(panel_owner, block_row, block_col, basis, blocks)
    return jnp.transpose(result, (1, 0, 2))


def solution(mesh):
    return jax.shard_map(
        local,
        mesh=mesh,
        in_specs=(
            P(("grp", "col"), None, None),
            P(("grp", "col")),
            P(("grp", "col")),
            P(),
            P(("grp", "col"), None, None),
        ),
        out_specs=P("col", None, None),
        check_vma=False,
    )
```

```python
import jax
import jax.numpy as jnp
from jax import lax
from jax.experimental import pallas as pl
from jax.experimental.pallas import tpu as pltpu
from jax.sharding import PartitionSpec as P

X, Y, Z, ZH, CORES = 4, 4, 8, 2, 2
RING = Z * ZH
BS, MODES, STEPS, CL, RUN = 320, 512, 2, 4, 8
PAD = 384
W2 = STEPS * BS
CHUNKS = 10
CH = BS // CHUNKS
PIECES = 10
PC = BS // PIECES
PH = PC // 2
T = STEPS * CHUNKS
G = STEPS * PIECES
SKEW = 5
AHEAD = 5
LEAD = 5
WP = 8
WR = MODES // WP
HM = MODES // CORES
W_AT = 8
WH = WR // 2
W_GO, W_STEP, W_LAG = 11, 3, 5
W_SUM = 46
EARLY = 56
COLS = X * Z
NH = 2
BF, F32 = jnp.bfloat16, jnp.float32


class Here:
    def __init__(self):
        grp, col = lax.axis_index("grp"), lax.axis_index("col")
        self.core, self.y, self.zh = grp % CORES, (grp // CORES) % Y, grp // (CORES * Y)
        self.z, self.x = col // X, col % X
        self.zg = self.zh * Z + self.z

    def at(self, zh=None, y=None, core=None, z=None, x=None):
        zh = self.zh if zh is None else zh
        y = self.y if y is None else y
        core = self.core if core is None else core
        z = self.z if z is None else z
        x = self.x if x is None else x
        return ((zh * Y + y) * CORES + core, z * X + x)

    def ring(self, d):
        p = (self.zg + d) % RING
        return self.at(zh=p // Z, z=p % Z)


def send(src, dst, ssem, rsem, dev):
    pltpu.make_async_remote_copy(
        src_ref=src, dst_ref=dst, send_sem=ssem, recv_sem=rsem,
        device_id=dev, device_id_type=pl.DeviceIdType.MESH,
    ).start()


def drain(ref, sem):
    pltpu.make_async_copy(ref, ref, sem).wait()


def greet(peers):
    barrier = pltpu.get_barrier_semaphore()
    for dev in peers:
        pl.semaphore_signal(barrier, inc=1, device_id=dev, device_id_type=pl.DeviceIdType.MESH)
    return barrier


def body(
    owner, brow, bcol, basis, blocks, out,
    blk, dense, basis_t, w_own, w_out, w_tr, w_tl, w_in, w_sum, w_pass,
    got, tr, tl, up_in, dn_in, up_out, dn_out, q,
    mine, kept, theirs, b3, z_in, out_all,
    blk_sem, s_x, s_tr, s_rl, s_z, s_w, s_c, s_q, s_p, s_zz, s_out,
    r_right, r_left, r_tr, r_tl, r_fr, r_fl, r_up, r_dn, r_wtr, r_wtl, r_w, r_c, r_q, r_p, r_zz, r_out,
):
    here = Here()
    core, x, y, z, zh, zg, at, ring = here.core, here.x, here.y, here.z, here.zh, here.zg, here.at, here.ring
    xr, xl, xo = (x + 1) % X, (x + 3) % X, (x + 2) % X
    right, left, other = at(x=xr), at(x=xl), at(core=1 - core)
    above, below = at(z=(z + 1) % Z), at(z=(z + Z - 1) % Z)
    plane = [(dx, dy) for dx in range(X) for dy in range(Y) if dx or dy]
    copies = [(dh, dy, dc) for dh in range(ZH) for dy in range(Y) for dc in range(CORES) if dh or dy or dc]

    fetch = pltpu.make_async_copy(blocks, blk, blk_sem)
    fetch.start()

    def copy_at(dh, dy, dc):
        return (zh + dh) % ZH, (y + dy) % Y, (core + dc) % CORES

    peers = [at(x=(x + dx) % X, y=(y + dy) % Y) for dx, dy in plane]
    peers += [ring(d) for d in range(1, RING)]
    for dh, dy, dc in copies:
        if dc or (dh and dy):
            hh, yy, cc = copy_at(dh, dy, dc)
            peers.append(at(zh=hh, y=yy, core=cc))
    barrier = greet(peers)
    got[0] = basis[x]
    for g in range(CORES):
        q[g, 0, BS:] = jnp.zeros((PAD - BS, MODES), BF)
        q[g, 1, : PAD - BS] = jnp.zeros((PAD - BS, MODES), BF)
    pl.semaphore_wait(barrier, len(peers))

    def piece(k):
        start = k * PC
        return (
            pl.ds(pl.multiple_of(start, PC), PC),
            pl.ds(pl.multiple_of(start, PH), PH),
            pl.ds(pl.multiple_of(start + PH, PH), PH),
            pl.ds(pl.multiple_of(k * PH, PH), PH),
        )

    def offer(k):
        rows, first, second, half = piece(k)
        send(basis.at[xo, first], tr.at[half], s_tr.at[0], r_tr.at[k], right)
        send(basis.at[xo, second], tl.at[half], s_tr.at[1], r_tl.at[k], left)
        send(basis.at[xr, rows], got.at[3, rows], s_x.at[0], r_right.at[k], right)
        send(basis.at[xl, rows], got.at[1, rows], s_x.at[1], r_left.at[k], left)

    for k in range(AHEAD):
        offer(k)
    def turn(m):
        lanes = pl.ds(pl.multiple_of(m * 128, 128), 128)
        flipped = basis[:, :, lanes].reshape(CL * BS, 128).astype(F32).T.reshape(8, CORES, 8, CL * BS)
        for k in range(CORES):
            rows = pl.ds(pl.multiple_of(k * HM + m * 64, 64), 64)
            basis_t[rows] = flipped[:, k].reshape(64, CL * BS).astype(BF)

    def place(s, r, c):
        where, found = jnp.int32(0), jnp.int32(0)
        for b in range(RUN):
            hit = (brow[s * RUN + b] % CL == r) & (bcol[s * RUN + b] % CL == c)
            where = jnp.where(hit, b, where)
            found = jnp.where(hit, 1, found)
        one = blk[s * RUN + where]
        one = jnp.where(found > 0, one, jnp.zeros_like(one))
        dense[c, pl.ds(pl.multiple_of(r * BS, BS), BS), s * BS : (s + 1) * BS] = one

    def multiply(c):
        return jnp.dot(basis_t[...], dense[c], preferred_element_type=F32)

    fetch.wait()

    def project(s, n):
        cols = slice(s * 256, s * 256 + PAD)
        part = jnp.zeros((HM, 256), F32)
        for g in range(CORES):
            panel = q[g, s, :, n * 256 : (n + 1) * 256]
            for t in range(2):
                part += jnp.dot(w_sum[g, t, :, cols], panel, preferred_element_type=F32)
        part = part.reshape(COLS, 8, 256)
        for i in range(X):
            both = jnp.concatenate([part[zz * X + i] for zz in range(Z)], axis=0)

            @pl.when(i == x)
            def _():
                for j in range(2):
                    kept[s, n * 2 + j] = both[:, j * 128 : (j + 1) * 128]

            both = both.astype(BF)
            for j in range(2):
                mine[s, i, n * 2 + j] = both[:, j * 128 : (j + 1) * 128]

    def over_plane(s):
        for i, (dx, dy) in enumerate(plane):
            xx, yy = (x + dx) % X, (y + dy) % Y
            send(mine.at[s, xx, yy], theirs.at[s, x, y], s_p.at[s, i], r_p.at[s, x * Y + y], at(x=xx, y=yy))

    owner_x = [owner[s] % X for s in range(STEPS)]
    owner_z = [owner[s] // X for s in range(STEPS)]
    far = jnp.maximum(z, Z - 1 - z)

    def pick(s, values):
        return jnp.where(s == 0, values[0], values[1])

    reach = LEAD + SKEW * far

    @pl.loop(0, LEAD + SKEW * (Z - 1) + T)
    def _(slot):
        @pl.when(slot < PIECES)
        def _():
            rows, first, second, half = piece(slot)
            drain(tr.at[half], r_tr.at[slot])
            send(tr.at[half], got.at[2, first], s_rl.at[0], r_fr.at[slot], right)
            drain(tl.at[half], r_tl.at[slot])
            send(tl.at[half], got.at[2, second], s_rl.at[1], r_fl.at[slot], left)

        @pl.when(slot < PIECES - AHEAD)
        def _():
            offer(slot + AHEAD)

        tg = slot - LEAD
        @pl.when((tg >= 0) & (tg < PIECES))
        def _():
            rows, first, second, half = piece(tg)
            drain(got.at[3, rows], r_right.at[tg])
            drain(got.at[1, rows], r_left.at[tg])
            drain(got.at[2, first], r_fr.at[tg])
            drain(got.at[2, second], r_fl.at[tg])

        def stream(t, inn, outt, rsem, ssem, has_in, has_out, dev):
            s, k = t // CHUNKS, t % CHUNKS
            rows = pl.ds(pl.multiple_of(k * CH, CH), CH)
            gap = (pick(s, owner_x) + X - x) % X
            own = got[0, rows]
            for d in range(1, X):
                own = jnp.where(gap == d, got[d, rows], own)

            @pl.when(has_in)
            def _():
                drain(inn.at[s, rows], rsem.at[t])
                outt[s, rows] = jnp.where(pick(s, owner_z) == z, own, inn[s, rows])

            @pl.when(jnp.logical_not(has_in))
            def _():
                outt[s, rows] = own

            @pl.when(has_out)
            def _():
                send(outt.at[s, rows], inn.at[s, rows], ssem, rsem.at[t], dev)

        tu = slot - LEAD - SKEW * z
        @pl.when((tu >= 0) & (tu < T))
        def _():
            stream(tu, up_in, up_out, r_up, s_z.at[0], z > 0, z < Z - 1, above)

        td = slot - LEAD - SKEW * (Z - 1 - z)
        @pl.when((td >= 0) & (td < T))
        def _():
            stream(td, dn_in, dn_out, r_dn, s_z.at[1], z < Z - 1, z > 0, below)

        tq = slot - reach
        @pl.when((tq >= 0) & (tq < T))
        def _():
            s, k = tq // CHUNKS, tq % CHUNKS
            rows = pl.ds(pl.multiple_of(k * CH, CH), CH)
            here_rows = pl.ds(pl.multiple_of(s * (PAD - BS) + k * CH, CH), CH)
            q[core, s, here_rows] = jnp.where(pick(s, owner_z) <= z, up_out[s, rows], dn_out[s, rows])


            send(q.at[core, s, here_rows], q.at[core, s, here_rows], s_q, r_q.at[s], other)

        tw = slot - W_GO
        @pl.when((tw >= 0) & (tw % W_STEP == 0) & (tw < WP * W_STEP))
        def _():
            k = tw // W_STEP
            rows = pl.ds(pl.multiple_of(k * WR, WR), WR)
            first = pl.ds(pl.multiple_of(k * WH, WH), WH)
            second = pl.ds(pl.multiple_of(MODES // 2 + k * WH, WH), WH)
            send(w_out.at[1, first], w_tr.at[first], s_w.at[0], r_wtr.at[k], right)
            send(w_out.at[1, second], w_tl.at[first], s_w.at[1], r_wtl.at[k], left)
            send(w_out.at[0, rows], w_in.at[0, rows], s_w.at[2], r_w.at[0], right)
            send(w_out.at[2, rows], w_in.at[2, rows], s_w.at[3], r_w.at[1], left)

        tv = slot - W_GO - W_LAG
        @pl.when((tv >= 0) & (tv % W_STEP == 0) & (tv < WP * W_STEP))
        def _():
            k = tv // W_STEP
            first = pl.ds(pl.multiple_of(k * WH, WH), WH)
            second = pl.ds(pl.multiple_of(MODES // 2 + k * WH, WH), WH)
            drain(w_tr.at[first], r_wtr.at[k])
            send(w_tr.at[first], w_in.at[1, first], s_w.at[4], r_w.at[2], right)
            drain(w_tl.at[first], r_wtl.at[k])
            send(w_tl.at[first], w_in.at[1, second], s_w.at[5], r_w.at[3], left)

        @pl.when(slot < 4)
        def _():
            turn(slot)

        @pl.when(slot < 8)
        def _():
            for i in range(2):
                for s in range(STEPS):
                    place(s, slot % CL, slot // CL * 2 + i)

        for i, d in enumerate((2, 1, 3)):
            @pl.when(slot == W_AT + i)
            def _(d=d):
                w_out[d - 1] = multiply((x + d) % X).astype(BF)

        @pl.when(slot == W_AT + 3)
        def _():
            w_own[...] = multiply(x)

        @pl.when(slot == W_SUM)
        def _():
            drain(w_in.at[0], r_w.at[0])
            drain(w_in.at[2], r_w.at[1])
            drain(w_in.at[1, : MODES // 2], r_w.at[2])
            drain(w_in.at[1, MODES // 2 :], r_w.at[3])

        @pl.when((slot >= W_SUM) & (slot < W_SUM + HM // 64))
        def _():
            m = slot - W_SUM
            to = pl.ds(pl.multiple_of(m * 64, 64), 64)
            for k in range(CORES):
                rows = pl.ds(pl.multiple_of(k * HM + m * 64, 64), 64)
                total = w_own[rows]
                for d in range(X - 1):
                    total += w_in[d, rows].astype(F32)
                big = total.astype(BF)
                small = (total - big.astype(F32)).astype(BF)

                @pl.when(core == k)
                def _():
                    w_sum[core, 0, to] = big
                    w_sum[core, 1, to] = small

                @pl.when(core != k)
                def _():
                    w_pass[0, to] = big
                    w_pass[1, to] = small

        @pl.when(slot == W_SUM + HM // 64 - 1)
        def _():
            send(w_pass, w_sum.at[core], s_c, r_c, other)

        @pl.when(slot == EARLY)
        def _():
            drain(w_sum.at[0], r_c)
            drain(up_in.at[0], r_q.at[0])
            project(0, 0)

        @pl.when(slot == EARLY + 1)
        def _():
            project(0, 1)
            over_plane(0)

    def over_z():
        for s in range(STEPS):
            total = kept[s, y]
            for dx, dy in plane:
                xx, yy = (x + dx) % X, (y + dy) % Y
                drain(theirs.at[s, xx, yy], r_p.at[s, xx * Y + yy])
                total += theirs[s, xx, yy].astype(F32)
            for zz in range(Z):
                b3[s, zz] = total[zz * 8 : (zz + 1) * 8]
        for d in range(1, RING):
            p = (zg + d) % RING
            send(b3.at[p // Z, p % Z], z_in.at[zg], s_zz.at[d - 1], r_zz.at[zg], ring(d))
        z_in[zg] = b3[zh, z]

    def spread():
        for d in range(1, RING):
            p = (zg + d) % RING
            drain(z_in.at[p], r_zz.at[p])
        total = z_in[0]
        for p in range(1, RING):
            total += z_in[p]
        out_all[zh, y, core] = total
        for i, (dh, dy, dc) in enumerate(copies):
            hh, yy, cc = copy_at(dh, dy, dc)
            send(
                out_all.at[zh, y, core], out_all.at[zh, y, core], s_out.at[i],
                r_out.at[(zh * Y + y) * CORES + core], at(zh=hh, y=yy, core=cc),
            )

    def finish():
        for dh, dy, dc in copies:
            hh, yy, cc = copy_at(dh, dy, dc)
            drain(out_all.at[hh, yy, cc], r_out.at[(hh * Y + yy) * CORES + cc])
        for s in range(STEPS):
            for k in range(CORES):
                for j in range(Y):
                    out[s, k * 8 : (k + 1) * 8, j * 128 : (j + 1) * 128] = out_all[s, j, k]

    drain(up_in.at[1], r_q.at[1])
    project(1, 0)
    project(1, 1)
    over_plane(1)

    drain(basis.at[xr], s_x.at[0])
    drain(basis.at[xl], s_x.at[1])
    for i in range(2):
        drain(tr, s_tr.at[i])
        drain(tr, s_rl.at[i])

    @pl.when(z < Z - 1)
    def _():
        drain(up_out, s_z.at[0])

    @pl.when(z > 0)
    def _():
        drain(dn_out, s_z.at[1])

    for i in (0, 1, 4, 5):
        drain(w_tr, s_w.at[i])
    drain(w_out.at[0], s_w.at[2])
    drain(w_out.at[2], s_w.at[3])
    drain(w_pass, s_c)
    drain(up_in, s_q)

    over_z()
    for s in range(STEPS):
        for i in range(len(plane)):
            drain(mine.at[s, 0, 0], s_p.at[s, i])
    spread()
    for d in range(RING - 1):
        drain(z_in.at[0], s_zz.at[d])
    finish()
    for i in range(len(copies)):
        drain(z_in.at[0], s_out.at[i])


def local(blocks, block_row, block_col, panel_owner, basis):
    dma = pltpu.SemaphoreType.DMA
    vmem = pltpu.VMEM
    scratch = [
        vmem((STEPS * RUN, BS, BS), BF),
        vmem((CL, CL * BS, W2), BF),
        vmem((MODES, CL * BS), BF),
        vmem((MODES, W2), F32),
        vmem((X - 1, MODES, W2), BF),
        vmem((MODES // 2, W2), BF),
        vmem((MODES // 2, W2), BF),
        vmem((X - 1, MODES, W2), BF),
        vmem((CORES, 2, HM, W2), BF),
        vmem((2, HM, W2), BF),
        vmem((X, BS, MODES), BF),
        vmem((BS // 2, MODES), BF),
        vmem((BS // 2, MODES), BF),
        vmem((STEPS, BS, MODES), BF),
        vmem((STEPS, BS, MODES), BF),
        vmem((STEPS, BS, MODES), BF),
        vmem((STEPS, BS, MODES), BF),
        vmem((CORES, STEPS, PAD, MODES), BF),
        vmem((STEPS, X, Y, 8 * Z, 128), BF),
        vmem((STEPS, Y, 8 * Z, 128), F32),
        vmem((STEPS, X, Y, 8 * Z, 128), BF),
        vmem((STEPS, Z, 8, 128), F32),
        vmem((RING, 8, 128), F32),
        vmem((STEPS, Y, CORES, 8, 128), F32),
        dma, dma((2,)), dma((2,)), dma((2,)), dma((2,)), dma((6,)), dma, dma,
        dma((STEPS, X * Y - 1)), dma((RING - 1,)), dma((ZH * Y * CORES - 1,)),
        dma((PIECES,)), dma((PIECES,)), dma((PIECES,)), dma((PIECES,)), dma((PIECES,)), dma((PIECES,)),
        dma((T,)), dma((T,)), dma((WP,)), dma((WP,)), dma((4,)), dma, dma((STEPS,)), dma((STEPS, X * Y)), dma((RING,)), dma((ZH * Y * CORES,)),
    ]
    smem = pl.BlockSpec(memory_space=pltpu.SMEM)
    whole = pl.BlockSpec(memory_space=pltpu.VMEM)
    result = pl.pallas_call(
        body,
        out_shape=jax.ShapeDtypeStruct((STEPS, CORES * 8, MODES), F32),
        in_specs=[smem, smem, smem, whole, pl.BlockSpec(memory_space=pl.ANY)],
        out_specs=whole,
        scratch_shapes=scratch,
        compiler_params=pltpu.CompilerParams(
            collective_id=0, has_side_effects=True, vmem_limit_bytes=56 * 1024 * 1024
        ),
        cost_estimate=pl.CostEstimate(flops=4_000_000_000, bytes_accessed=5_000_000, transcendentals=0),
        name="galerkin",
    )(panel_owner, block_row, block_col, basis, blocks)
    return jnp.transpose(result, (1, 0, 2))


def solution(mesh):
    return jax.shard_map(
        local,
        mesh=mesh,
        in_specs=(
            P(("grp", "col"), None, None),
            P(("grp", "col")),
            P(("grp", "col")),
            P(),
            P(("grp", "col"), None, None),
        ),
        out_specs=P("col", None, None),
        check_vma=False,
    )
```

```python
import jax
import jax.numpy as jnp
from jax import lax
from jax.experimental import pallas as pl
from jax.experimental.pallas import tpu as pltpu
from jax.sharding import PartitionSpec as P

X, Y, Z, ZH, CORES = 4, 4, 8, 2, 2
RING = Z * ZH
BS, MODES, STEPS, CL, RUN = 320, 512, 2, 4, 8
PAD = 384
W2 = STEPS * BS
CHUNKS = 10
CH = BS // CHUNKS
PIECES = 10
PC = BS // PIECES
T = STEPS * CHUNKS
G = STEPS * PIECES
SKEW = 4
AHEAD = 5
WP = 8
WR = MODES // WP
HM = MODES // CORES
W_AT = 8
W_GO = 11
W_SUM = 38
EARLY = 44
COLS = X * Z
NH = 2
BF, F32 = jnp.bfloat16, jnp.float32


class Here:
    def __init__(self):
        grp, col = lax.axis_index("grp"), lax.axis_index("col")
        self.core, self.y, self.zh = grp % CORES, (grp // CORES) % Y, grp // (CORES * Y)
        self.z, self.x = col // X, col % X
        self.zg = self.zh * Z + self.z

    def at(self, zh=None, y=None, core=None, z=None, x=None):
        zh = self.zh if zh is None else zh
        y = self.y if y is None else y
        core = self.core if core is None else core
        z = self.z if z is None else z
        x = self.x if x is None else x
        return ((zh * Y + y) * CORES + core, z * X + x)

    def ring(self, d):
        p = (self.zg + d) % RING
        return self.at(zh=p // Z, z=p % Z)


def send(src, dst, ssem, rsem, dev):
    pltpu.make_async_remote_copy(
        src_ref=src, dst_ref=dst, send_sem=ssem, recv_sem=rsem,
        device_id=dev, device_id_type=pl.DeviceIdType.MESH,
    ).start()


def drain(ref, sem):
    pltpu.make_async_copy(ref, ref, sem).wait()


def greet(peers):
    barrier = pltpu.get_barrier_semaphore()
    for dev in peers:
        pl.semaphore_signal(barrier, inc=1, device_id=dev, device_id_type=pl.DeviceIdType.MESH)
    return barrier


def body(
    owner, brow, bcol, basis, blocks, out,
    blk, dense, basis_t, w_own, w_out, w_in, w_sum, w_pass,
    got, up_in, dn_in, up_out, dn_out, q,
    mine, kept, theirs, b3, z_in, out_all,
    blk_sem, s_x, s_z, s_w, s_c, s_q, s_p, s_zz, s_out,
    r_x, r_up, r_dn, r_w, r_c, r_q, r_p, r_zz, r_out,
):
    here = Here()
    core, x, y, z, zh, zg, at, ring = here.core, here.x, here.y, here.z, here.zh, here.zg, here.at, here.ring
    xr, xl, xo = (x + 1) % X, (x + 3) % X, (x + 2) % X
    right, left, other = at(x=xr), at(x=xl), at(core=1 - core)
    above, below = at(z=(z + 1) % Z), at(z=(z + Z - 1) % Z)
    plane = [(dx, dy) for dx in range(X) for dy in range(Y) if dx or dy]
    copies = [(dh, dy, dc) for dh in range(ZH) for dy in range(Y) for dc in range(CORES) if dh or dy or dc]

    fetch = pltpu.make_async_copy(blocks, blk, blk_sem)
    fetch.start()

    def copy_at(dh, dy, dc):
        return (zh + dh) % ZH, (y + dy) % Y, (core + dc) % CORES

    peers = [at(x=(x + dx) % X, y=(y + dy) % Y) for dx, dy in plane]
    peers += [ring(d) for d in range(1, RING)]
    for dh, dy, dc in copies:
        if dc or (dh and dy):
            hh, yy, cc = copy_at(dh, dy, dc)
            peers.append(at(zh=hh, y=yy, core=cc))
    barrier = greet(peers)
    got[0] = basis[x]
    for g in range(CORES):
        q[g, 0, BS:] = jnp.zeros((PAD - BS, MODES), BF)
        q[g, 1, : PAD - BS] = jnp.zeros((PAD - BS, MODES), BF)
    pl.semaphore_wait(barrier, len(peers))

    def offer(k):
        rows = pl.ds(pl.multiple_of(k * PC, PC), PC)
        for d, dev in ((2, at(x=xo)), (1, right), (3, left)):
            send(basis.at[(x + d) % X, rows], got.at[X - d, rows], s_x.at[d - 1], r_x.at[d - 1, k], dev)

    for k in range(AHEAD):
        offer(k)
    def turn(m):
        lanes = pl.ds(pl.multiple_of(m * 128, 128), 128)
        flipped = basis[:, :, lanes].reshape(CL * BS, 128).astype(F32).T.reshape(8, CORES, 8, CL * BS)
        for k in range(CORES):
            rows = pl.ds(pl.multiple_of(k * HM + m * 64, 64), 64)
            basis_t[rows] = flipped[:, k].reshape(64, CL * BS).astype(BF)

    def place(s, r, c):
        where, found = jnp.int32(0), jnp.int32(0)
        for b in range(RUN):
            hit = (brow[s * RUN + b] % CL == r) & (bcol[s * RUN + b] % CL == c)
            where = jnp.where(hit, b, where)
            found = jnp.where(hit, 1, found)
        one = blk[s * RUN + where]
        one = jnp.where(found > 0, one, jnp.zeros_like(one))
        dense[c, pl.ds(pl.multiple_of(r * BS, BS), BS), s * BS : (s + 1) * BS] = one

    def multiply(c):
        return jnp.dot(basis_t[...], dense[c], preferred_element_type=F32)

    fetch.wait()

    def project(s, n):
        cols = slice(s * 256, s * 256 + PAD)
        part = jnp.zeros((HM, 256), F32)
        for g in range(CORES):
            panel = q[g, s, :, n * 256 : (n + 1) * 256]
            for t in range(2):
                part += jnp.dot(w_sum[g, t, :, cols], panel, preferred_element_type=F32)
        part = part.reshape(COLS, 8, 256)
        for i in range(X):
            both = jnp.concatenate([part[zz * X + i] for zz in range(Z)], axis=0)

            @pl.when(i == x)
            def _():
                for j in range(2):
                    kept[s, n * 2 + j] = both[:, j * 128 : (j + 1) * 128]

            both = both.astype(BF)
            for j in range(2):
                mine[s, i, n * 2 + j] = both[:, j * 128 : (j + 1) * 128]

    def over_plane(s):
        for i, (dx, dy) in enumerate(plane):
            xx, yy = (x + dx) % X, (y + dy) % Y
            send(mine.at[s, xx, yy], theirs.at[s, x, y], s_p.at[s, i], r_p.at[s, x * Y + y], at(x=xx, y=yy))

    owner_x = [owner[s] % X for s in range(STEPS)]
    owner_z = [owner[s] // X for s in range(STEPS)]
    far = jnp.maximum(z, Z - 1 - z)

    def pick(s, values):
        return jnp.where(s == 0, values[0], values[1])

    reach = SKEW * far

    @pl.loop(0, SKEW * (Z - 1) + T)
    def _(slot):
        @pl.when(slot < PIECES - AHEAD)
        def _():
            offer(slot + AHEAD)

        @pl.when(slot < PIECES)
        def _():
            rows = pl.ds(pl.multiple_of(slot * PC, PC), PC)
            for d in range(1, X):
                drain(got.at[X - d, rows], r_x.at[d - 1, slot])

        def stream(t, inn, outt, rsem, ssem, has_in, has_out, dev):
            s, k = t // CHUNKS, t % CHUNKS
            rows = pl.ds(pl.multiple_of(k * CH, CH), CH)
            gap = (pick(s, owner_x) + X - x) % X
            own = got[0, rows]
            for d in range(1, X):
                own = jnp.where(gap == d, got[d, rows], own)

            @pl.when(has_in)
            def _():
                drain(inn.at[s, rows], rsem.at[t])
                outt[s, rows] = jnp.where(pick(s, owner_z) == z, own, inn[s, rows])

            @pl.when(jnp.logical_not(has_in))
            def _():
                outt[s, rows] = own

            @pl.when(has_out)
            def _():
                send(outt.at[s, rows], inn.at[s, rows], ssem, rsem.at[t], dev)

        tu = slot - SKEW * z
        @pl.when((tu >= 0) & (tu < T))
        def _():
            stream(tu, up_in, up_out, r_up, s_z.at[0], z > 0, z < Z - 1, above)

        td = slot - SKEW * (Z - 1 - z)
        @pl.when((td >= 0) & (td < T))
        def _():
            stream(td, dn_in, dn_out, r_dn, s_z.at[1], z < Z - 1, z > 0, below)

        tq = slot - reach
        @pl.when((tq >= 0) & (tq < T))
        def _():
            s, k = tq // CHUNKS, tq % CHUNKS
            rows = pl.ds(pl.multiple_of(k * CH, CH), CH)
            here_rows = pl.ds(pl.multiple_of(s * (PAD - BS) + k * CH, CH), CH)
            q[core, s, here_rows] = jnp.where(pick(s, owner_z) <= z, up_out[s, rows], dn_out[s, rows])


            send(q.at[core, s, here_rows], q.at[core, s, here_rows], s_q, r_q.at[s], other)

        tw = slot - W_GO
        for i, (d, dev) in enumerate(((2, at(x=xo)), (1, right), (3, left))):
            @pl.when((tw >= 0) & (tw % (X - 1) == i) & (tw < WP * (X - 1)))
            def _(d=d, dev=dev):
                rows = pl.ds(pl.multiple_of(tw // (X - 1) * WR, WR), WR)
                send(w_out.at[d - 1, rows], w_in.at[d - 1, rows], s_w.at[d - 1], r_w.at[d - 1], dev)

        @pl.when(slot < 4)
        def _():
            turn(slot)

        @pl.when(slot < 8)
        def _():
            for i in range(2):
                for s in range(STEPS):
                    place(s, slot % CL, slot // CL * 2 + i)

        for i, d in enumerate((2, 1, 3)):
            @pl.when(slot == W_AT + i)
            def _(d=d):
                w_out[d - 1] = multiply((x + d) % X).astype(BF)

        @pl.when(slot == W_AT + 3)
        def _():
            w_own[...] = multiply(x)

        @pl.when(slot == W_SUM)
        def _():
            for d in range(X - 1):
                drain(w_in.at[d], r_w.at[d])

        @pl.when((slot >= W_SUM) & (slot < W_SUM + HM // 64))
        def _():
            m = slot - W_SUM
            to = pl.ds(pl.multiple_of(m * 64, 64), 64)
            for k in range(CORES):
                rows = pl.ds(pl.multiple_of(k * HM + m * 64, 64), 64)
                total = w_own[rows]
                for d in range(X - 1):
                    total += w_in[d, rows].astype(F32)
                big = total.astype(BF)
                small = (total - big.astype(F32)).astype(BF)

                @pl.when(core == k)
                def _():
                    w_sum[core, 0, to] = big
                    w_sum[core, 1, to] = small

                @pl.when(core != k)
                def _():
                    w_pass[0, to] = big
                    w_pass[1, to] = small

        @pl.when(slot == W_SUM + HM // 64 - 1)
        def _():
            send(w_pass, w_sum.at[core], s_c, r_c, other)

        @pl.when(slot == EARLY)
        def _():
            drain(w_sum.at[0], r_c)
            drain(up_in.at[0], r_q.at[0])
            project(0, 0)

        @pl.when(slot == EARLY + 1)
        def _():
            project(0, 1)
            over_plane(0)

    def over_z():
        for s in range(STEPS):
            total = kept[s, y]
            for dx, dy in plane:
                xx, yy = (x + dx) % X, (y + dy) % Y
                drain(theirs.at[s, xx, yy], r_p.at[s, xx * Y + yy])
                total += theirs[s, xx, yy].astype(F32)
            for zz in range(Z):
                b3[s, zz] = total[zz * 8 : (zz + 1) * 8]
        for d in range(1, RING):
            p = (zg + d) % RING
            send(b3.at[p // Z, p % Z], z_in.at[zg], s_zz.at[d - 1], r_zz.at[zg], ring(d))
        z_in[zg] = b3[zh, z]

    def spread():
        for d in range(1, RING):
            p = (zg + d) % RING
            drain(z_in.at[p], r_zz.at[p])
        total = z_in[0]
        for p in range(1, RING):
            total += z_in[p]
        out_all[zh, y, core] = total
        for i, (dh, dy, dc) in enumerate(copies):
            hh, yy, cc = copy_at(dh, dy, dc)
            send(
                out_all.at[zh, y, core], out_all.at[zh, y, core], s_out.at[i],
                r_out.at[(zh * Y + y) * CORES + core], at(zh=hh, y=yy, core=cc),
            )

    def finish():
        for dh, dy, dc in copies:
            hh, yy, cc = copy_at(dh, dy, dc)
            drain(out_all.at[hh, yy, cc], r_out.at[(hh * Y + yy) * CORES + cc])
        for s in range(STEPS):
            for k in range(CORES):
                for j in range(Y):
                    out[s, k * 8 : (k + 1) * 8, j * 128 : (j + 1) * 128] = out_all[s, j, k]

    drain(up_in.at[1], r_q.at[1])
    project(1, 0)
    project(1, 1)
    over_plane(1)

    for d in range(X - 1):
        drain(basis.at[d], s_x.at[d])

    @pl.when(z < Z - 1)
    def _():
        drain(up_out, s_z.at[0])

    @pl.when(z > 0)
    def _():
        drain(dn_out, s_z.at[1])

    for d in range(X - 1):
        drain(w_out.at[d], s_w.at[d])
    drain(w_pass, s_c)
    drain(up_in, s_q)

    over_z()
    for s in range(STEPS):
        for i in range(len(plane)):
            drain(mine.at[s, 0, 0], s_p.at[s, i])
    spread()
    for d in range(RING - 1):
        drain(z_in.at[0], s_zz.at[d])
    finish()
    for i in range(len(copies)):
        drain(z_in.at[0], s_out.at[i])


def local(blocks, block_row, block_col, panel_owner, basis):
    dma = pltpu.SemaphoreType.DMA
    vmem = pltpu.VMEM
    scratch = [
        vmem((STEPS * RUN, BS, BS), BF),
        vmem((CL, CL * BS, W2), BF),
        vmem((MODES, CL * BS), BF),
        vmem((MODES, W2), F32),
        vmem((X - 1, MODES, W2), BF),
        vmem((X - 1, MODES, W2), BF),
        vmem((CORES, 2, HM, W2), BF),
        vmem((2, HM, W2), BF),
        vmem((X, BS, MODES), BF),
        vmem((STEPS, BS, MODES), BF),
        vmem((STEPS, BS, MODES), BF),
        vmem((STEPS, BS, MODES), BF),
        vmem((STEPS, BS, MODES), BF),
        vmem((CORES, STEPS, PAD, MODES), BF),
        vmem((STEPS, X, Y, 8 * Z, 128), BF),
        vmem((STEPS, Y, 8 * Z, 128), F32),
        vmem((STEPS, X, Y, 8 * Z, 128), BF),
        vmem((STEPS, Z, 8, 128), F32),
        vmem((RING, 8, 128), F32),
        vmem((STEPS, Y, CORES, 8, 128), F32),
        dma, dma((X - 1,)), dma((2,)), dma((X - 1,)), dma, dma,
        dma((STEPS, X * Y - 1)), dma((RING - 1,)), dma((ZH * Y * CORES - 1,)),
        dma((X - 1, PIECES)),
        dma((T,)), dma((T,)), dma((X - 1,)), dma, dma((STEPS,)), dma((STEPS, X * Y)), dma((RING,)), dma((ZH * Y * CORES,)),
    ]
    smem = pl.BlockSpec(memory_space=pltpu.SMEM)
    whole = pl.BlockSpec(memory_space=pltpu.VMEM)
    result = pl.pallas_call(
        body,
        out_shape=jax.ShapeDtypeStruct((STEPS, CORES * 8, MODES), F32),
        in_specs=[smem, smem, smem, whole, pl.BlockSpec(memory_space=pl.ANY)],
        out_specs=whole,
        scratch_shapes=scratch,
        compiler_params=pltpu.CompilerParams(
            collective_id=0, has_side_effects=True, vmem_limit_bytes=56 * 1024 * 1024
        ),
        cost_estimate=pl.CostEstimate(flops=4_000_000_000, bytes_accessed=5_000_000, transcendentals=0),
        name="galerkin",
    )(panel_owner, block_row, block_col, basis, blocks)
    return jnp.transpose(result, (1, 0, 2))


def solution(mesh):
    return jax.shard_map(
        local,
        mesh=mesh,
        in_specs=(
            P(("grp", "col"), None, None),
            P(("grp", "col")),
            P(("grp", "col")),
            P(),
            P(("grp", "col"), None, None),
        ),
        out_specs=P("col", None, None),
        check_vma=False,
    )
```

```python
import jax
import jax.numpy as jnp
from jax import lax
from jax.experimental import pallas as pl
from jax.experimental.pallas import tpu as pltpu
from jax.sharding import PartitionSpec as P

X, Y, Z, ZH, CORES = 4, 4, 8, 2, 2
RING = Z * ZH
BS, MODES, STEPS, CL, RUN = 320, 512, 2, 4, 8
PAD = 384
W2 = STEPS * BS
CHUNKS = 10
CH = BS // CHUNKS
PIECES = 10
PC = BS // PIECES
PH = PC // 2
T = STEPS * CHUNKS
G = STEPS * PIECES
SKEW = 5
AHEAD = 5
LEAD = 5
WP = 8
WR = MODES // WP
HM = MODES // CORES
W_AT = 8
WH = WR // 2
W_GO, W_STEP, W_LAG = 11, 3, 12
W_SUM = 52
COLS = X * Z
NH = 2
BF, F32 = jnp.bfloat16, jnp.float32


class Here:
    def __init__(self):
        grp, col = lax.axis_index("grp"), lax.axis_index("col")
        self.core, self.y, self.zh = grp % CORES, (grp // CORES) % Y, grp // (CORES * Y)
        self.z, self.x = col // X, col % X
        self.zg = self.zh * Z + self.z

    def at(self, zh=None, y=None, core=None, z=None, x=None):
        zh = self.zh if zh is None else zh
        y = self.y if y is None else y
        core = self.core if core is None else core
        z = self.z if z is None else z
        x = self.x if x is None else x
        return ((zh * Y + y) * CORES + core, z * X + x)

    def ring(self, d):
        p = (self.zg + d) % RING
        return self.at(zh=p // Z, z=p % Z)


def send(src, dst, ssem, rsem, dev):
    pltpu.make_async_remote_copy(
        src_ref=src, dst_ref=dst, send_sem=ssem, recv_sem=rsem,
        device_id=dev, device_id_type=pl.DeviceIdType.MESH,
    ).start()


def drain(ref, sem):
    pltpu.make_async_copy(ref, ref, sem).wait()


def greet(peers):
    barrier = pltpu.get_barrier_semaphore()
    for dev in peers:
        pl.semaphore_signal(barrier, inc=1, device_id=dev, device_id_type=pl.DeviceIdType.MESH)
    return barrier


def body(
    owner, brow, bcol, basis, blocks, out,
    blk, dense, basis_t, w_own, w_out, w_tr, w_tl, w_in, w_sum, w_pass,
    got, tr, tl, up_in, dn_in, up_out, dn_out, q,
    mine, kept, theirs, b3, z_in, out_all,
    blk_sem, s_x, s_tr, s_rl, s_z, s_w, s_c, s_q, s_p, s_zz, s_out,
    r_right, r_left, r_tr, r_tl, r_fr, r_fl, r_up, r_dn, r_wtr, r_wtl, r_w, r_c, r_q, r_p, r_zz, r_out,
):
    here = Here()
    core, x, y, z, zh, zg, at, ring = here.core, here.x, here.y, here.z, here.zh, here.zg, here.at, here.ring
    xr, xl, xo = (x + 1) % X, (x + 3) % X, (x + 2) % X
    right, left, other = at(x=xr), at(x=xl), at(core=1 - core)
    above, below = at(z=(z + 1) % Z), at(z=(z + Z - 1) % Z)
    plane = [(dx, dy) for dx in range(X) for dy in range(Y) if dx or dy]
    copies = [(dh, dy, dc) for dh in range(ZH) for dy in range(Y) for dc in range(CORES) if dh or dy or dc]

    fetch = pltpu.make_async_copy(blocks, blk, blk_sem)
    fetch.start()

    def copy_at(dh, dy, dc):
        return (zh + dh) % ZH, (y + dy) % Y, (core + dc) % CORES

    peers = [at(x=(x + dx) % X, y=(y + dy) % Y) for dx, dy in plane]
    peers += [ring(d) for d in range(1, RING)]
    for dh, dy, dc in copies:
        if dc or (dh and dy):
            hh, yy, cc = copy_at(dh, dy, dc)
            peers.append(at(zh=hh, y=yy, core=cc))
    barrier = greet(peers)
    got[0] = basis[x]
    for g in range(CORES):
        q[g, 0, BS:] = jnp.zeros((PAD - BS, MODES), BF)
        q[g, 1, : PAD - BS] = jnp.zeros((PAD - BS, MODES), BF)
    pl.semaphore_wait(barrier, len(peers))

    def piece(k):
        start = k * PC
        return (
            pl.ds(pl.multiple_of(start, PC), PC),
            pl.ds(pl.multiple_of(start, PH), PH),
            pl.ds(pl.multiple_of(start + PH, PH), PH),
            pl.ds(pl.multiple_of(k * PH, PH), PH),
        )

    def offer(k):
        rows, first, second, half = piece(k)
        send(basis.at[xo, first], tr.at[half], s_tr.at[0], r_tr.at[k], right)
        send(basis.at[xo, second], tl.at[half], s_tr.at[1], r_tl.at[k], left)
        send(basis.at[xr, rows], got.at[3, rows], s_x.at[0], r_right.at[k], right)
        send(basis.at[xl, rows], got.at[1, rows], s_x.at[1], r_left.at[k], left)

    for k in range(AHEAD):
        offer(k)
    def turn(m):
        lanes = pl.ds(pl.multiple_of(m * 128, 128), 128)
        flipped = basis[:, :, lanes].reshape(CL * BS, 128).astype(F32).T.reshape(8, CORES, 8, CL * BS)
        for k in range(CORES):
            rows = pl.ds(pl.multiple_of(k * HM + m * 64, 64), 64)
            basis_t[rows] = flipped[:, k].reshape(64, CL * BS).astype(BF)

    def place(s, r, c):
        where, found = jnp.int32(0), jnp.int32(0)
        for b in range(RUN):
            hit = (brow[s * RUN + b] % CL == r) & (bcol[s * RUN + b] % CL == c)
            where = jnp.where(hit, b, where)
            found = jnp.where(hit, 1, found)
        one = blk[s * RUN + where]
        one = jnp.where(found > 0, one, jnp.zeros_like(one))
        dense[c, pl.ds(pl.multiple_of(r * BS, BS), BS), s * BS : (s + 1) * BS] = one

    def multiply(c):
        return jnp.dot(basis_t[...], dense[c], preferred_element_type=F32)

    fetch.wait()

    def project(s, n):
        cols = slice(s * 256, s * 256 + PAD)
        part = jnp.zeros((HM, 256), F32)
        for g in range(CORES):
            panel = q[g, s, :, n * 256 : (n + 1) * 256]
            for t in range(2):
                part += jnp.dot(w_sum[g, t, :, cols], panel, preferred_element_type=F32)
        part = part.reshape(COLS, 8, 256)
        for i in range(X):
            both = jnp.concatenate([part[zz * X + i] for zz in range(Z)], axis=0)

            @pl.when(i == x)
            def _():
                for j in range(2):
                    kept[s, n * 2 + j] = both[:, j * 128 : (j + 1) * 128]

            both = both.astype(BF)
            for j in range(2):
                mine[s, i, n * 2 + j] = both[:, j * 128 : (j + 1) * 128]

    def over_plane(s):
        for i, (dx, dy) in enumerate(plane):
            xx, yy = (x + dx) % X, (y + dy) % Y
            send(mine.at[s, xx, yy], theirs.at[s, x, y], s_p.at[s, i], r_p.at[s, x * Y + y], at(x=xx, y=yy))

    owner_x = [owner[s] % X for s in range(STEPS)]
    owner_z = [owner[s] // X for s in range(STEPS)]
    far = jnp.maximum(z, Z - 1 - z)

    def pick(s, values):
        return jnp.where(s == 0, values[0], values[1])

    reach = LEAD + SKEW * far

    @pl.loop(0, LEAD + SKEW * (Z - 1) + T)
    def _(slot):
        @pl.when(slot < PIECES)
        def _():
            rows, first, second, half = piece(slot)
            drain(tr.at[half], r_tr.at[slot])
            send(tr.at[half], got.at[2, first], s_rl.at[0], r_fr.at[slot], right)
            drain(tl.at[half], r_tl.at[slot])
            send(tl.at[half], got.at[2, second], s_rl.at[1], r_fl.at[slot], left)

        @pl.when(slot < PIECES - AHEAD)
        def _():
            offer(slot + AHEAD)

        tg = slot - LEAD
        @pl.when((tg >= 0) & (tg < PIECES))
        def _():
            rows, first, second, half = piece(tg)
            drain(got.at[3, rows], r_right.at[tg])
            drain(got.at[1, rows], r_left.at[tg])
            drain(got.at[2, first], r_fr.at[tg])
            drain(got.at[2, second], r_fl.at[tg])

        def stream(t, inn, outt, rsem, ssem, has_in, has_out, dev):
            s, k = t // CHUNKS, t % CHUNKS
            rows = pl.ds(pl.multiple_of(k * CH, CH), CH)
            gap = (pick(s, owner_x) + X - x) % X
            own = got[0, rows]
            for d in range(1, X):
                own = jnp.where(gap == d, got[d, rows], own)

            @pl.when(has_in)
            def _():
                drain(inn.at[s, rows], rsem.at[t])
                outt[s, rows] = jnp.where(pick(s, owner_z) == z, own, inn[s, rows])

            @pl.when(jnp.logical_not(has_in))
            def _():
                outt[s, rows] = own

            @pl.when(has_out)
            def _():
                send(outt.at[s, rows], inn.at[s, rows], ssem, rsem.at[t], dev)

        tu = slot - LEAD - SKEW * z
        @pl.when((tu >= 0) & (tu < T))
        def _():
            stream(tu, up_in, up_out, r_up, s_z.at[0], z > 0, z < Z - 1, above)

        td = slot - LEAD - SKEW * (Z - 1 - z)
        @pl.when((td >= 0) & (td < T))
        def _():
            stream(td, dn_in, dn_out, r_dn, s_z.at[1], z < Z - 1, z > 0, below)

        tq = slot - reach
        @pl.when((tq >= 0) & (tq < T))
        def _():
            s, k = tq // CHUNKS, tq % CHUNKS
            rows = pl.ds(pl.multiple_of(k * CH, CH), CH)
            here_rows = pl.ds(pl.multiple_of(s * (PAD - BS) + k * CH, CH), CH)
            q[core, s, here_rows] = jnp.where(pick(s, owner_z) <= z, up_out[s, rows], dn_out[s, rows])


            send(q.at[core, s, here_rows], q.at[core, s, here_rows], s_q, r_q.at[s], other)

        tw = slot - W_GO
        @pl.when((tw >= 0) & (tw % W_STEP == 0) & (tw < WP * W_STEP))
        def _():
            k = tw // W_STEP
            rows = pl.ds(pl.multiple_of(k * WR, WR), WR)
            first = pl.ds(pl.multiple_of(k * WH, WH), WH)
            second = pl.ds(pl.multiple_of(MODES // 2 + k * WH, WH), WH)
            send(w_out.at[1, first], w_tr.at[first], s_w.at[0], r_wtr.at[k], right)
            send(w_out.at[1, second], w_tl.at[first], s_w.at[1], r_wtl.at[k], left)
            send(w_out.at[0, rows], w_in.at[0, rows], s_w.at[2], r_w.at[0], right)
            send(w_out.at[2, rows], w_in.at[2, rows], s_w.at[3], r_w.at[1], left)

        tv = slot - W_GO - W_LAG
        @pl.when((tv >= 0) & (tv % W_STEP == 0) & (tv < WP * W_STEP))
        def _():
            k = tv // W_STEP
            first = pl.ds(pl.multiple_of(k * WH, WH), WH)
            second = pl.ds(pl.multiple_of(MODES // 2 + k * WH, WH), WH)
            drain(w_tr.at[first], r_wtr.at[k])
            send(w_tr.at[first], w_in.at[1, first], s_w.at[4], r_w.at[2], right)
            drain(w_tl.at[first], r_wtl.at[k])
            send(w_tl.at[first], w_in.at[1, second], s_w.at[5], r_w.at[3], left)

        @pl.when(slot < 4)
        def _():
            turn(slot)

        @pl.when(slot < 8)
        def _():
            for i in range(2):
                for s in range(STEPS):
                    place(s, slot % CL, slot // CL * 2 + i)

        for i, d in enumerate((2, 1, 3)):
            @pl.when(slot == W_AT + i)
            def _(d=d):
                w_out[d - 1] = multiply((x + d) % X).astype(BF)

        @pl.when(slot == W_AT + 3)
        def _():
            w_own[...] = multiply(x)

        @pl.when(slot == W_SUM)
        def _():
            drain(w_in.at[0], r_w.at[0])
            drain(w_in.at[2], r_w.at[1])
            drain(w_in.at[1, : MODES // 2], r_w.at[2])
            drain(w_in.at[1, MODES // 2 :], r_w.at[3])

        @pl.when((slot >= W_SUM) & (slot < W_SUM + HM // 64))
        def _():
            m = slot - W_SUM
            to = pl.ds(pl.multiple_of(m * 64, 64), 64)
            for k in range(CORES):
                rows = pl.ds(pl.multiple_of(k * HM + m * 64, 64), 64)
                total = w_own[rows]
                for d in range(X - 1):
                    total += w_in[d, rows].astype(F32)
                big = total.astype(BF)
                small = (total - big.astype(F32)).astype(BF)

                @pl.when(core == k)
                def _():
                    w_sum[core, 0, to] = big
                    w_sum[core, 1, to] = small

                @pl.when(core != k)
                def _():
                    w_pass[0, to] = big
                    w_pass[1, to] = small

        @pl.when(slot == W_SUM + HM // 64 - 1)
        def _():
            send(w_pass, w_sum.at[core], s_c, r_c, other)

    def over_z():
        for s in range(STEPS):
            total = kept[s, y]
            for dx, dy in plane:
                xx, yy = (x + dx) % X, (y + dy) % Y
                drain(theirs.at[s, xx, yy], r_p.at[s, xx * Y + yy])
                total += theirs[s, xx, yy].astype(F32)
            for zz in range(Z):
                b3[s, zz] = total[zz * 8 : (zz + 1) * 8]
        for d in range(1, RING):
            p = (zg + d) % RING
            send(b3.at[p // Z, p % Z], z_in.at[zg], s_zz.at[d - 1], r_zz.at[zg], ring(d))
        z_in[zg] = b3[zh, z]

    def spread():
        for d in range(1, RING):
            p = (zg + d) % RING
            drain(z_in.at[p], r_zz.at[p])
        total = z_in[0]
        for p in range(1, RING):
            total += z_in[p]
        out_all[zh, y, core] = total
        for i, (dh, dy, dc) in enumerate(copies):
            hh, yy, cc = copy_at(dh, dy, dc)
            send(
                out_all.at[zh, y, core], out_all.at[zh, y, core], s_out.at[i],
                r_out.at[(zh * Y + y) * CORES + core], at(zh=hh, y=yy, core=cc),
            )

    def finish():
        for dh, dy, dc in copies:
            hh, yy, cc = copy_at(dh, dy, dc)
            drain(out_all.at[hh, yy, cc], r_out.at[(hh * Y + yy) * CORES + cc])
        for s in range(STEPS):
            for k in range(CORES):
                for j in range(Y):
                    out[s, k * 8 : (k + 1) * 8, j * 128 : (j + 1) * 128] = out_all[s, j, k]

    drain(w_sum.at[0], r_c)
    drain(up_in.at[0], r_q.at[0])
    project(0, 0)
    project(0, 1)
    over_plane(0)
    drain(up_in.at[1], r_q.at[1])
    project(1, 0)
    project(1, 1)
    over_plane(1)

    drain(basis.at[xr], s_x.at[0])
    drain(basis.at[xl], s_x.at[1])
    for i in range(2):
        drain(tr, s_tr.at[i])
        drain(tr, s_rl.at[i])

    @pl.when(z < Z - 1)
    def _():
        drain(up_out, s_z.at[0])

    @pl.when(z > 0)
    def _():
        drain(dn_out, s_z.at[1])

    for i in (0, 1, 4, 5):
        drain(w_tr, s_w.at[i])
    drain(w_out.at[0], s_w.at[2])
    drain(w_out.at[2], s_w.at[3])
    drain(w_pass, s_c)
    drain(up_in, s_q)

    over_z()
    for s in range(STEPS):
        for i in range(len(plane)):
            drain(mine.at[s, 0, 0], s_p.at[s, i])
    spread()
    for d in range(RING - 1):
        drain(z_in.at[0], s_zz.at[d])
    finish()
    for i in range(len(copies)):
        drain(z_in.at[0], s_out.at[i])


def local(blocks, block_row, block_col, panel_owner, basis):
    dma = pltpu.SemaphoreType.DMA
    vmem = pltpu.VMEM
    scratch = [
        vmem((STEPS * RUN, BS, BS), BF),
        vmem((CL, CL * BS, W2), BF),
        vmem((MODES, CL * BS), BF),
        vmem((MODES, W2), F32),
        vmem((X - 1, MODES, W2), BF),
        vmem((MODES // 2, W2), BF),
        vmem((MODES // 2, W2), BF),
        vmem((X - 1, MODES, W2), BF),
        vmem((CORES, 2, HM, W2), BF),
        vmem((2, HM, W2), BF),
        vmem((X, BS, MODES), BF),
        vmem((BS // 2, MODES), BF),
        vmem((BS // 2, MODES), BF),
        vmem((STEPS, BS, MODES), BF),
        vmem((STEPS, BS, MODES), BF),
        vmem((STEPS, BS, MODES), BF),
        vmem((STEPS, BS, MODES), BF),
        vmem((CORES, STEPS, PAD, MODES), BF),
        vmem((STEPS, X, Y, 8 * Z, 128), BF),
        vmem((STEPS, Y, 8 * Z, 128), F32),
        vmem((STEPS, X, Y, 8 * Z, 128), BF),
        vmem((STEPS, Z, 8, 128), F32),
        vmem((RING, 8, 128), F32),
        vmem((STEPS, Y, CORES, 8, 128), F32),
        dma, dma((2,)), dma((2,)), dma((2,)), dma((2,)), dma((6,)), dma, dma,
        dma((STEPS, X * Y - 1)), dma((RING - 1,)), dma((ZH * Y * CORES - 1,)),
        dma((PIECES,)), dma((PIECES,)), dma((PIECES,)), dma((PIECES,)), dma((PIECES,)), dma((PIECES,)),
        dma((T,)), dma((T,)), dma((WP,)), dma((WP,)), dma((4,)), dma, dma((STEPS,)), dma((STEPS, X * Y)), dma((RING,)), dma((ZH * Y * CORES,)),
    ]
    smem = pl.BlockSpec(memory_space=pltpu.SMEM)
    whole = pl.BlockSpec(memory_space=pltpu.VMEM)
    result = pl.pallas_call(
        body,
        out_shape=jax.ShapeDtypeStruct((STEPS, CORES * 8, MODES), F32),
        in_specs=[smem, smem, smem, whole, pl.BlockSpec(memory_space=pl.ANY)],
        out_specs=whole,
        scratch_shapes=scratch,
        compiler_params=pltpu.CompilerParams(
            collective_id=0, has_side_effects=True, vmem_limit_bytes=56 * 1024 * 1024
        ),
        cost_estimate=pl.CostEstimate(flops=4_000_000_000, bytes_accessed=5_000_000, transcendentals=0),
        name="galerkin",
    )(panel_owner, block_row, block_col, basis, blocks)
    return jnp.transpose(result, (1, 0, 2))


def solution(mesh):
    return jax.shard_map(
        local,
        mesh=mesh,
        in_specs=(
            P(("grp", "col"), None, None),
            P(("grp", "col")),
            P(("grp", "col")),
            P(),
            P(("grp", "col"), None, None),
        ),
        out_specs=P("col", None, None),
        check_vma=False,
    )
```
